512 devices in a mesh: exp: 64 (over z, x), patch: 8 (over y, core).
Axes of the slice: x: 4, y: 4, z: 16, core: 2. Of those that a mesh axis runs over, the one named last changes fastest.
Arguments:
- image: float32 [64, 1024, 512], P('exp', 'patch'), may hold values from -8 to 8
- row_taps: float32 [20, 41], replicated, may hold values from -1 to 1
- col_taps: float32 [20, 41], replicated, may hold values from -1 to 1
- coefficients: float32 [64, 20], P('exp'), may hold values from -1.5 to 1.5
- exposure_weight: float32 [64], P('exp'), may hold values from 0.25 to 4
- warp_offset: int32 [64, 8, 32], P('exp', 'patch'), may hold values from 0 to 16
- target_cell: int32 [64, 8, 32, 1], P('exp', 'patch'), may hold values from 0 to 63, as said below
Outputs:
- coadd: float32 [8, 64, 16, 128], P('patch', 'exp')
The draws below stay inside these ranges and needn't reach their ends.
Inputs may be any that keep to these rules, and one draw needn't show every extreme that they name: `target_cell`: no exposure sends more than 2 of its tiles on one patch to one cell, and each exposure sends exactly 2 to some cell of every patch; on every patch one cell receives exactly 2 tiles from every exposure, and every cell receives at least one tile.
All inputs are finite; a program needn't handle non-finite values.
Results may differ from the reference program's by a relative error of at most 0.00012.
Values sent between devices are 32-bit elements; how exact they have to be, the bound alone decides.
A program may use at most 64 MiB of HBM per device.

```python
import math
import jax
import jax.numpy as jnp
from jax import lax

NB = 20
TAPS = 41
HALF = 20
ROWS_DEV = 128
COLS = 512
TR = 16
TW = 128
SHIFT = 8
TILES_DEV = 32
CAP = 2
EXPOSURES = 64
PATCHES = 8
CELLS = 64
ROWS = 1024


def draw_target_cell(key, part):
    key = jax.random.fold_in(key, 7)
    keys = jax.random.split(key, 4)
    rank = jax.vmap(lambda sub: jax.random.permutation(sub, CELLS))(jax.random.split(keys[0], PATCHES)).astype(jnp.int32)
    hottest = jnp.argsort(rank, axis=1)[:, 0].astype(jnp.int32)
    offset = jax.random.randint(keys[1], (PATCHES,), 0, CELLS, dtype=jnp.int32)
    expo_ids = jnp.arange(EXPOSURES, dtype=jnp.int32)[:, None]
    forced = (expo_ids + offset[None, :]) % CELLS
    noise = jax.random.randint(keys[2], (EXPOSURES, PATCHES, CELLS), 0, CELLS, dtype=jnp.int32)
    cell_ids = jnp.arange(CELLS, dtype=jnp.int32)
    score = (rank[None, :, :] + noise) * CELLS + rank[None, :, :]
    score = jnp.where(cell_ids[None, None, :] == hottest[None, :, None], -1, score)
    score = jnp.where(cell_ids[None, None, :] == forced[:, :, None], -2, score)
    order = jnp.argsort(score, axis=-1).astype(jnp.int32)
    counts = jax.random.randint(keys[3], (EXPOSURES, PATCHES, CELLS), CAP // 2, CAP + 1, dtype=jnp.int32)
    counts = jnp.where(cell_ids[None, None, :] < 2, CAP, counts).astype(jnp.int32)
    ends = jnp.cumsum(counts, axis=-1).astype(jnp.int32)
    tile_ids = jnp.arange(TILES_DEV, dtype=jnp.int32)
    placed = jnp.sum((ends[:, :, None, :] <= tile_ids[None, None, :, None]).astype(jnp.int32), axis=-1)
    chosen = jnp.take_along_axis(order, placed.astype(jnp.int32), axis=-1)
    return chosen[..., None].astype(jnp.int32)


def set_ends(values, own_key, least, high):
    longest = values.shape.index(max(values.shape))
    spots = []
    for shift in (0, 1):
        where = [jax.random.randint(jax.random.fold_in(own_key, axis), (), 0, length) for axis, length in enumerate(values.shape)]
        where[longest] = (where[longest] + shift) % values.shape[longest]
        spots.append(tuple(where))
    return values.at[spots[0]].set(least).at[spots[1]].set(high)


def level_of(stream_key, dims, pieces, low, high):
    gain, own = 1.0, jax.random.fold_in(stream_key, 6)
    for dim, shards_of in pieces:
        steps = jnp.exp(jax.random.uniform(jax.random.fold_in(own, dim), (shards_of,), jnp.float32, low / len(pieces), high / len(pieces)))
        gain = gain * jnp.repeat(steps, dims[dim] // shards_of).reshape([-1 if axis == dim else 1 for axis in range(len(dims))])
    return gain


def gaussian(stream_key, dims, scale, bound, pieces=(), kind=jnp.bfloat16):
    values = scale * jax.random.normal(stream_key, dims, jnp.float32)
    if pieces:
        values = values * level_of(stream_key, dims, pieces, -0.22, 0.18)
    return jnp.clip(values, -bound, bound).astype(kind)


def setup_inputs(seed: int = 0) -> dict:
    arg_keys = jax.random.split(jax.random.key(seed), 8)
    return {
        "image": gaussian(arg_keys[0], (EXPOSURES, ROWS, COLS), 1.0, 8.0, ((0, 64), (1, 8)), jnp.float32),
        "row_taps": gaussian(arg_keys[1], (NB, TAPS), TAPS ** -0.5, 1.0, (), jnp.float32),
        "col_taps": gaussian(arg_keys[2], (NB, TAPS), TAPS ** -0.5, 1.0, (), jnp.float32),
        "coefficients": gaussian(arg_keys[3], (EXPOSURES, NB), 0.25, 1.5, ((0, 64),), jnp.float32),
        "exposure_weight": jnp.clip(jnp.exp(math.log(4.0) - 2.7725887 * jax.random.uniform(arg_keys[4], (EXPOSURES,), jnp.float32) ** level_of(arg_keys[4], (EXPOSURES,), ((0, 64),), -0.2, 0.2)), 0.25, 4.0),
        "warp_offset": set_ends(jax.random.randint(arg_keys[5], (EXPOSURES, PATCHES, TILES_DEV), 0, 2 * SHIFT + 1), jax.random.fold_in(arg_keys[5], 1), 0, 2 * SHIFT).astype(jnp.int32),
        "target_cell": draw_target_cell(jax.random.fold_in(arg_keys[7], 71), 0),
    }


def match_one(picture, coeff_row, row_taps, col_taps):
    lhs = picture[None, None, :, :]
    horiz = row_taps[:, None, None, :]
    spread = lax.conv_general_dilated(lhs, horiz, (1, 1), ((0, 0), (HALF, HALF)), precision=lax.Precision.HIGHEST)
    vert = (coeff_row[:, None] * col_taps)[None, :, :, None]
    joined = lax.conv_general_dilated(spread, vert, (1, 1), ((HALF, HALF), (0, 0)), precision=lax.Precision.HIGHEST)
    return joined[0, 0]


def reference(image, row_taps, col_taps, coefficients, exposure_weight, warp_offset, target_cell):
    matched = lax.map(lambda pair: match_one(pair[0], pair[1], row_taps, col_taps), (image, coefficients))
    padded = jnp.pad(matched, ((0, 0), (0, 0), (SHIFT, SHIFT)))
    per_row = COLS // TW
    expo_ids = jnp.arange(EXPOSURES, dtype=jnp.int32)[:, None, None] + jnp.zeros((1, PATCHES, TILES_DEV), jnp.int32)
    patch_ids = jnp.arange(PATCHES, dtype=jnp.int32)[None, :, None] + jnp.zeros((EXPOSURES, 1, TILES_DEV), jnp.int32)
    tile_ids = jnp.arange(TILES_DEV, dtype=jnp.int32)[None, None, :] + jnp.zeros((EXPOSURES, PATCHES, 1), jnp.int32)
    row_start = (patch_ids * ROWS_DEV + (tile_ids // per_row) * TR).astype(jnp.int32)
    col_start = ((tile_ids % per_row) * TW + warp_offset).astype(jnp.int32)

    def cut(expo, row0, col0):
        return lax.dynamic_slice(padded, (expo, row0, col0), (1, TR, TW))[0]

    tiles = jax.vmap(cut)(expo_ids.reshape(-1), row_start.reshape(-1), col_start.reshape(-1))
    weights = (exposure_weight[:, None, None] + jnp.zeros((1, PATCHES, TILES_DEV), jnp.float32)).reshape(-1)
    segment = (patch_ids * CELLS + target_cell[..., 0]).reshape(-1)
    numer = jax.ops.segment_sum(weights[:, None, None] * tiles, segment, num_segments=PATCHES * CELLS)
    denom = jax.ops.segment_sum(weights, segment, num_segments=PATCHES * CELLS)
    return (numer / denom[:, None, None]).reshape(PATCHES, CELLS, TR, TW)
```

```python
import functools

import jax
import jax.numpy as jnp
from jax import lax
from jax.experimental import pallas as pl
from jax.experimental.pallas import tpu as pltpu
from jax.sharding import PartitionSpec as P

NB = 20
TAPS = 41
HALF = 20
NROWS = 128
NCOLS = 512
TR = 16
TW = 128
SHIFT = 8
NTILES = 32
NX = 4
PAD = 24
F32 = jnp.float32
BF16 = jnp.bfloat16
MESH = pl.DeviceIdType.MESH
ROWQ = 4
XB = 64
NJ = NCOLS // XB
NA = (ROWQ + TAPS + ROWQ - 2) // ROWQ
NKAP = NA * ROWQ
NQ = NROWS // ROWQ
NG = 48


def lanes(rows):
    return lax.broadcasted_iota(jnp.int32, (rows, 128), 1)


def build_patterns(coef_ref, row_ref, col_ref, scaled, rhi, rlo):
    for b in range(NB):
        scaled[b : b + 1, :] = col_ref[b : b + 1, :] * coef_ref[0, b]
    tap = lax.broadcasted_iota(jnp.int32, (TAPS, 128), 0)
    place = lax.broadcasted_iota(jnp.int32, (TAPS, 128), 1)
    flip = jnp.where((XB - place % XB) % XB == tap, 1.0, 0.0).astype(F32)
    rowpat = jnp.dot(row_ref[...], flip, precision=lax.Precision.HIGHEST, preferred_element_type=F32)
    pats = lax.dot_general(
        scaled[...], rowpat, (((0,), (0,)), ((), ())), precision=lax.Precision.HIGHEST, preferred_element_type=F32
    )
    gap = lax.broadcasted_iota(jnp.int32, (128, 128), 0) - lanes(128) % XB
    keep = (gap >= 0) & (gap < TAPS)
    for i in range(TAPS):
        base = jnp.broadcast_to(pats[i : i + 1, :], (XB, 128))
        ring = pltpu.roll(base, 0, 1, stride=1, stride_axis=0)
        band = jnp.where(keep, jnp.concatenate([ring, ring], axis=0), 0.0)
        high = band.astype(BF16)
        rhi[i + ROWQ - 1] = high
        rlo[i + ROWQ - 1] = (band - high.astype(F32)).astype(BF16)
    zero = jnp.zeros((128, 128), BF16)
    for i in list(range(ROWQ - 1)) + list(range(TAPS + ROWQ - 1, NKAP + ROWQ - 1)):
        rhi[i] = zero
        rlo[i] = zero


def build_weights(rhi, rlo, whi, wlo):
    left = lanes(128) < XB

    def one(kappa, carry):
        rows = pl.ds(pl.multiple_of(kappa * 128, 128), 128)
        for src, dst in ((rhi, whi), (rlo, wlo)):
            dst[rows, 0:128] = jnp.where(left, src[kappa + 3], src[kappa + 2])
            dst[rows, 128:256] = jnp.where(left, src[kappa + 1], src[kappa])
        return carry

    lax.fori_loop(0, NKAP, one, 0)


def build_planes(buf, phi, plo):
    lane = lanes(NG)

    def one(rho, carry):
        cols = [buf[j, pl.ds(rho, NG, stride=ROWQ), :] for j in range(4)]
        zero = jnp.zeros((NG, 128), F32)
        padded = [zero] + cols + [zero]
        for j in range(4):
            even = jnp.where(lane < HALF, pltpu.roll(padded[j], HALF, 1), pltpu.roll(padded[j + 1], HALF, 1))
            odd = jnp.where(
                lane < XB + HALF, pltpu.roll(padded[j + 1], XB + HALF, 1), pltpu.roll(padded[j + 2], XB + HALF, 1)
            )
            for place, part in ((2 * j, even), (2 * j + 1, odd)):
                high = part.astype(BF16).astype(F32)
                phi[rho, place] = high
                plo[rho, place] = part - high
        return carry

    lax.fori_loop(0, ROWQ, one, 0)


def convolve(phi, plo, whi, wlo, acc):
    total = None
    for a in range(NA):
        def lhs(src):
            return jnp.concatenate(
                [
                    jnp.concatenate([src[rho, j, a + 1 : a + 1 + NQ, :].astype(BF16) for j in range(NJ)], axis=0)
                    for rho in range(ROWQ)
                ],
                axis=1,
            )

        high, low = lhs(phi), lhs(plo)
        rows = slice(a * 512, (a + 1) * 512)
        part = (
            jnp.dot(high, whi[rows, :], preferred_element_type=F32)
            + jnp.dot(low, whi[rows, :], preferred_element_type=F32)
            + jnp.dot(high, wlo[rows, :], preferred_element_type=F32)
        )
        if a == 0:
            acc[...] = part
        else:
            acc[...] += part


def to_matched(acc, mat, weight):
    left = lanes(NQ) < XB
    mat[0] = jnp.zeros((NROWS, 128), F32)
    mat[5] = jnp.zeros((NROWS, 128), F32)
    for j in range(4):
        for pair in range(2):
            cols = slice(pair * 128, pair * 128 + 128)
            even = acc[2 * j * NQ : (2 * j + 1) * NQ, cols] * weight
            odd = acc[(2 * j + 1) * NQ : (2 * j + 2) * NQ, cols] * weight
            mat[j + 1, pl.ds(2 * pair, NQ, stride=ROWQ), :] = jnp.where(left, even, pltpu.roll(odd, XB, 1))
            mat[j + 1, pl.ds(2 * pair + 1, NQ, stride=ROWQ), :] = jnp.where(left, pltpu.roll(even, XB, 1), odd)


def cut_tiles(offs_ref, mat, tiles):
    lane = lanes(TR)
    tiles[NTILES] = jnp.zeros((TR, 128), F32)

    def one(t, carry):
        rows = pl.ds(pl.multiple_of(t * TR, TR), TR)
        for q in range(4):
            off = offs_ref[0, t * 4 + q]
            side = jnp.where(off >= SHIFT, q + 2, q)
            turn = (128 + SHIFT - off) % 128
            own = pltpu.roll(mat[q + 1, rows, :], turn, 1)
            other = pltpu.roll(mat[side, rows, :], turn, 1)
            source = lane + (off - SHIFT)
            tiles[t * 4 + q] = jnp.where((source >= 0) & (source < 128), own, other)
        return carry

    lax.fori_loop(0, NROWS // TR, one, 0)


def gather_cells(slots, tiles, send, cells, h):
    rows = slice(h * 8, h * 8 + 8)

    def one(depth, carry):
        for x in range(NX):
            cell = depth * NX + x
            send[h, x, depth] = tiles[slots[0, cell], rows, :] + tiles[slots[1, cell], rows, :]
        return carry

    lax.fori_loop(0, cells // NX, one, 0)


def kernel(
    nz, npatch,
    offs_ref, cell_ref, coef_ref, wgt_ref, row_ref, col_ref, img_ref, out_ref,
    buf, scaled, rhi, rlo, whi, wlo, phi, plo, acc, mat, tiles,
    slotv, slots, denx, denz, send, recv_far, recv_near, xsum, recv_z,
    load_sem, slot_sem, halo_send, halo_recv, denx_send, denx_recv, denz_send, denz_recv,
    far_send, far_recv, near_send, near_recv, z_send, z_recv,
):
    cells = nz * NX
    half = nz // 2
    me, patch = lax.axis_index("exp"), lax.axis_index("patch")
    zpos, xpos = me // NX, me % NX
    right, left, across = (xpos + 1) % NX, (xpos + NX - 1) % NX, (xpos + 2) % NX
    barrier = pltpu.get_barrier_semaphore()

    def along_x(x):
        return (zpos * NX + x, patch)

    def along_z(d):
        return ((zpos + d) % nz * NX + xpos, patch)

    def load(j):
        return pltpu.make_async_copy(
            img_ref.at[:, pl.ds(j * 128, 128)], buf.at[j, pl.ds(PAD, NROWS), :], load_sem.at[j]
        )

    def halo(way):
        source, target = ((NROWS, 0), (PAD, PAD + NROWS))[way]
        return pltpu.make_async_remote_copy(
            src_ref=buf.at[:, pl.ds(source, PAD), :],
            dst_ref=buf.at[:, pl.ds(target, PAD), :],
            send_sem=halo_send.at[way],
            recv_sem=halo_recv.at[way],
            device_id=(me, patch + (1, -1)[way]),
            device_id_type=MESH,
        )

    def remote(src, dst, ssem, rsem, target):
        return pltpu.make_async_remote_copy(
            src_ref=src, dst_ref=dst, send_sem=ssem, recv_sem=rsem, device_id=target, device_id_type=MESH
        )

    def den_x(n):
        return remote(
            denx.at[0], denx.at[n], denx_send.at[n], denx_recv.at[n], along_x((xpos + n) % NX)
        )

    def den_z(d):
        return remote(denz.at[0], denz.at[d], denz_send.at[d], denz_recv.at[d], along_z(d))

    def far(h, way):
        return remote(
            send.at[h, across, pl.ds(way * half, half)],
            recv_far.at[h, way],
            far_send.at[2 * h + way],
            far_recv.at[2 * h + way],
            along_x((right, left)[way]),
        )

    def near(h, way, part):
        x = (right, left)[way]
        rows = pl.ds(part * half, half)
        place = 4 * h + 2 * way + part
        return remote(
            send.at[h, x, rows], recv_near.at[h, way, rows], near_send.at[place], near_recv.at[place], along_x(x)
        )

    def deep(h, d):
        return remote(
            xsum.at[h, (zpos + d) % nz], recv_z.at[h, d], z_send.at[h, d], z_recv.at[h, d], along_z(d)
        )

    def each(count, action):
        lax.fori_loop(1, count, lambda d, carry: (action(d), carry)[1], 0)

    for j in range(4):
        load(j).start()

    def greet(target):
        pl.semaphore_signal(barrier, inc=1, device_id=target, device_id_type=MESH)

    @pl.when(patch > 0)
    def _():
        greet((me, patch - 1))

    @pl.when(patch < npatch - 1)
    def _():
        greet((me, patch + 1))

    for n in range(1, NX):
        greet(along_x((xpos + n) % NX))
    each(nz, lambda d: greet(along_z(d)))

    lane = lax.broadcasted_iota(jnp.int32, (8, 128), 1)
    first = jnp.full((8, 128), NTILES, jnp.int32)
    last = jnp.full((8, 128), -1, jnp.int32)
    count = jnp.zeros((8, 128), F32)
    for k in range(NTILES):
        hit = lane == cell_ref[0, k]
        count = count + jnp.where(hit, 1.0, 0.0)
        first = jnp.minimum(first, jnp.where(hit, k, NTILES))
        last = jnp.maximum(last, jnp.where(hit, k, -1))
    sub = lax.broadcasted_iota(jnp.int32, (8, 128), 0)
    slotv[...] = jnp.where(sub == 0, first, jnp.where(last > first, last, NTILES))
    slot_copy = pltpu.make_async_copy(slotv, slots, slot_sem)
    slot_copy.start()
    denx[0] = (count * wgt_ref[0])[0:1]

    build_patterns(coef_ref, row_ref, col_ref, scaled, rhi, rlo)

    neighbours = jnp.where(patch > 0, 1, 0) + jnp.where(patch < npatch - 1, 1, 0)
    pl.semaphore_wait(barrier, neighbours + NX - 1 + nz - 1)
    for j in range(4):
        load(j).wait()

    @pl.when(patch < npatch - 1)
    def _():
        halo(0).start()

    @pl.when(patch > 0)
    def _():
        halo(1).start()

    for n in range(1, NX):
        den_x(n).start()

    @pl.when(patch == 0)
    def _():
        buf[:, 0:PAD, :] = jnp.zeros((4, PAD, 128), F32)

    @pl.when(patch == npatch - 1)
    def _():
        buf[:, PAD + NROWS : PAD + NROWS + PAD, :] = jnp.zeros((4, PAD, 128), F32)

    buf[:, PAD + NROWS + PAD :, :] = jnp.zeros((4, NG * ROWQ - NROWS - 2 * PAD, 128), F32)

    build_weights(rhi, rlo, whi, wlo)

    for n in range(1, NX):
        den_x(n).wait_recv()
    denz[0] = denx[0] + denx[1] + denx[2] + denx[3]
    each(nz, lambda d: den_z(d).start())

    @pl.when(patch > 0)
    def _():
        halo(0).wait_recv()

    @pl.when(patch < npatch - 1)
    def _():
        halo(1).wait_recv()

    build_planes(buf, phi, plo)
    convolve(phi, plo, whi, wlo, acc)
    to_matched(acc, mat, wgt_ref[0])
    cut_tiles(offs_ref, mat, tiles)
    slot_copy.wait()
    for h in range(2):
        gather_cells(slots, tiles, send, cells, h)
        for way in range(2):
            far(h, way).start()
        near(h, 0, 1).start()
        near(h, 1, 0).start()

    for h in range(2):
        for way in range(2):
            far(h, way).wait_recv()
            x = (right, left)[way]
            rows = pl.ds(way * half, half)
            send[h, x, rows] += recv_far[h, way]
            near(h, way, way).start()

    for h in range(2):
        for way in range(2):
            for part in range(2):
                near(h, way, part).wait_recv()
        xsum[h] = send[h, xpos] + recv_near[h, 0] + recv_near[h, 1]
        each(nz, lambda d: deep(h, d).start())

    each(nz, lambda d: den_z(d).wait_recv())
    den = denz[0]
    for d in range(1, nz):
        den = den + denz[d]
    den = jnp.sum(jnp.where(lanes(1) == me, den, 0.0), axis=1, keepdims=True)
    for h in range(2):
        def add(d, total):
            deep(h, d).wait_recv()
            return total + recv_z[h, d]

        total = lax.fori_loop(1, nz, add, xsum[h, zpos])
        out_ref[h * 8 : h * 8 + 8, :] = total / den

    @pl.when(patch < npatch - 1)
    def _():
        halo(0).wait_send()

    @pl.when(patch > 0)
    def _():
        halo(1).wait_send()

    for n in range(1, NX):
        den_x(n).wait_send()
    each(nz, lambda d: den_z(d).wait_send())
    for h in range(2):
        for way in range(2):
            far(h, way).wait_send()
            for part in range(2):
                near(h, way, part).wait_send()
        each(nz, lambda d: deep(h, d).wait_send())


def per_device(nz, npatch, image, row_taps, col_taps, coefficients, exposure_weight, warp_offset, target_cell):
    smem = pl.BlockSpec(memory_space=pltpu.SMEM)
    vmem = pl.BlockSpec(memory_space=pltpu.VMEM)
    half = nz // 2
    scratch = pltpu.VMEM
    dma = pltpu.SemaphoreType.DMA
    out = pl.pallas_call(
        functools.partial(kernel, nz, npatch),
        out_shape=jax.ShapeDtypeStruct((TR, TW), F32),
        in_specs=[smem, smem, smem, smem, vmem, vmem, pl.BlockSpec(memory_space=pl.ANY)],
        out_specs=vmem,
        scratch_shapes=[
            scratch((4, NG * ROWQ, 128), F32),
            scratch((NB, TAPS), F32),
            scratch((NKAP + ROWQ - 1, 128, 128), BF16),
            scratch((NKAP + ROWQ - 1, 128, 128), BF16),
            scratch((NKAP * 128, 256), BF16),
            scratch((NKAP * 128, 256), BF16),
            scratch((ROWQ, NJ, NG, 128), F32),
            scratch((ROWQ, NJ, NG, 128), F32),
            scratch((NJ * NQ, 256), F32),
            scratch((6, NROWS, 128), F32),
            scratch((NTILES + 1, TR, TW), F32),
            scratch((8, 128), jnp.int32),
            pltpu.SMEM((8, 128), jnp.int32),
            scratch((NX, 1, 128), F32),
            scratch((nz, 1, 128), F32),
            scratch((2, NX, nz, 8, 128), F32),
            scratch((2, 2, half, 8, 128), F32),
            scratch((2, 2, nz, 8, 128), F32),
            scratch((2, nz, 8, 128), F32),
            scratch((2, nz, 8, 128), F32),
            dma((4,)),
            dma,
            dma((2,)),
            dma((2,)),
            dma((NX,)),
            dma((NX,)),
            dma((nz,)),
            dma((nz,)),
            dma((4,)),
            dma((4,)),
            dma((8,)),
            dma((8,)),
            dma((2, nz)),
            dma((2, nz)),
        ],
        compiler_params=pltpu.CompilerParams(
            collective_id=0, has_side_effects=True, vmem_limit_bytes=48 * 2**20
        ),
    )(
        warp_offset.reshape(1, NTILES),
        target_cell.reshape(1, NTILES),
        coefficients,
        exposure_weight,
        row_taps,
        col_taps,
        image.reshape(NROWS, NCOLS),
    )
    return out[None, None]


def solution(mesh):
    nz = mesh.shape["exp"] // NX
    npatch = mesh.shape["patch"]
    return jax.shard_map(
        functools.partial(per_device, nz, npatch),
        mesh=mesh,
        in_specs=(
            P("exp", "patch", None),
            P(),
            P(),
            P("exp", None),
            P("exp"),
            P("exp", "patch", None),
            P("exp", "patch", None, None),
        ),
        out_specs=P("patch", "exp", None, None),
        check_vma=False,
    )
```

```python
import functools

import jax
import jax.numpy as jnp
from jax import lax
from jax.experimental import pallas as pl
from jax.experimental.pallas import tpu as pltpu
from jax.sharding import PartitionSpec as P

NB = 20
TAPS = 41
HALF = 20
NROWS = 128
NCOLS = 512
TR = 16
TW = 128
SHIFT = 8
NTILES = 32
NX = 4
PAD = 24
F32 = jnp.float32
BF16 = jnp.bfloat16
MESH = pl.DeviceIdType.MESH
ROWQ = 4
XB = 64
NJ = NCOLS // XB
NA = (ROWQ + TAPS + ROWQ - 2) // ROWQ
NKAP = NA * ROWQ
NQ = NROWS // ROWQ
NG = 48
NCHUNK = 4


def lanes(rows):
    return lax.broadcasted_iota(jnp.int32, (rows, 128), 1)


def build_weights(coef_ref, row_ref, col_ref, scaled, phigh, plow):
    for b in range(NB):
        scaled[b : b + 1, :] = col_ref[b : b + 1, :] * coef_ref[0, b]
    tap = lax.broadcasted_iota(jnp.int32, (TAPS, 128), 0)
    place = lax.broadcasted_iota(jnp.int32, (TAPS, 128), 1)
    flip = jnp.where((XB - place % XB) % XB == tap, 1.0, 0.0).astype(F32)
    rowpat = jnp.dot(row_ref[...], flip, precision=lax.Precision.HIGHEST, preferred_element_type=F32)
    pats = lax.dot_general(
        scaled[...], rowpat, (((0,), (0,)), ((), ())), precision=lax.Precision.HIGHEST, preferred_element_type=F32
    )
    left = lanes(XB) < XB
    gap = lax.broadcasted_iota(jnp.int32, (128, 128), 0) - lanes(128) % XB
    keep = (gap >= 0) & (gap < TAPS)
    zero = jnp.zeros((XB, 128), F32)
    rings = [zero] * (ROWQ - 1)
    for i in range(TAPS):
        base = jnp.broadcast_to(pats[i : i + 1, :], (XB, 128))
        rings.append(pltpu.roll(base, 0, 1, stride=1, stride_axis=0))
    rings += [zero] * ROWQ
    for kappa in range(-2, NKAP):
        pair = jnp.where(left, rings[kappa + 3], rings[kappa + 2])
        band = jnp.where(keep, jnp.concatenate([pair, pair], axis=0), 0.0)
        high = band.astype(BF16)
        rows = slice((kappa + 2) * 128, (kappa + 3) * 128)
        phigh[rows, :] = high
        plow[rows, :] = (band - high.astype(F32)).astype(BF16)


def build_planes(buf, phi, plo):
    lane = lanes(NG)

    def one(rho, carry):
        cols = [buf[j, pl.ds(rho, NG, stride=ROWQ), :] for j in range(4)]
        zero = jnp.zeros((NG, 128), F32)
        padded = [zero] + cols + [zero]
        for j in range(4):
            even = jnp.where(lane < HALF, pltpu.roll(padded[j], HALF, 1), pltpu.roll(padded[j + 1], HALF, 1))
            odd = jnp.where(
                lane < XB + HALF, pltpu.roll(padded[j + 1], XB + HALF, 1), pltpu.roll(padded[j + 2], XB + HALF, 1)
            )
            for place, part in ((2 * j, even), (2 * j + 1, odd)):
                high = part.astype(BF16).astype(F32)
                phi[rho, place] = high
                plo[rho, place] = part - high
        return carry

    lax.fori_loop(0, ROWQ, one, 0)


def convolve(steps, phi, plo, phigh, plow, acc):
    def lhs(src, a):
        return jnp.concatenate(
            [
                jnp.concatenate([src[rho, j, a + 1 : a + 1 + NQ, :].astype(BF16) for j in range(NJ)], axis=0)
                for rho in range(ROWQ)
            ],
            axis=1,
        )

    def rhs(src, a):
        return jnp.concatenate(
            [src[(a * ROWQ + 2) * 128 : (a * ROWQ + 6) * 128, :], src[a * ROWQ * 128 : (a * ROWQ + 4) * 128, :]], axis=1
        )

    def dot(x, y):
        return jnp.dot(x, y, preferred_element_type=F32)

    for a in steps:
        high, low = lhs(phi, a), lhs(plo, a)
        wide, fine = rhs(phigh, a), rhs(plow, a)
        part = dot(high, wide) + dot(low, wide) + dot(high, fine)
        if a == 0:
            acc[...] = part
        else:
            acc[...] += part


def to_matched(acc, mat, weight):
    left = lanes(NQ) < XB
    mat[0] = jnp.zeros((NROWS, 128), F32)
    mat[5] = jnp.zeros((NROWS, 128), F32)
    for j in range(4):
        for pair in range(2):
            cols = slice(pair * 128, pair * 128 + 128)
            even = acc[2 * j * NQ : (2 * j + 1) * NQ, cols] * weight
            odd = acc[(2 * j + 1) * NQ : (2 * j + 2) * NQ, cols] * weight
            mat[j + 1, pl.ds(2 * pair, NQ, stride=ROWQ), :] = jnp.where(left, even, pltpu.roll(odd, XB, 1))
            mat[j + 1, pl.ds(2 * pair + 1, NQ, stride=ROWQ), :] = jnp.where(left, pltpu.roll(even, XB, 1), odd)


def cut_tiles(offs_ref, mat, tiles):
    lane = lanes(TR)
    tiles[NTILES] = jnp.zeros((TR, 128), F32)

    def one(t, carry):
        rows = pl.ds(pl.multiple_of(t * TR, TR), TR)
        for q in range(4):
            off = offs_ref[0, t * 4 + q]
            side = jnp.where(off >= SHIFT, q + 2, q)
            turn = (128 + SHIFT - off) % 128
            own = pltpu.roll(mat[q + 1, rows, :], turn, 1)
            other = pltpu.roll(mat[side, rows, :], turn, 1)
            source = lane + (off - SHIFT)
            tiles[t * 4 + q] = jnp.where((source >= 0) & (source < 128), own, other)
        return carry

    lax.fori_loop(0, NROWS // TR, one, 0)


def kernel(
    nz, npatch,
    offs_hbm, cell_hbm, coef_hbm, wgt_hbm, row_hbm, col_hbm, img_hbm, out_ref,
    offs, cell, coef, wgt, rowt, colt,
    buf, scaled, phigh, plow, phi, plo, acc, mat, tiles,
    slotv, slots, denx, denz, send, recv_x, xsum, recv_z,
    load_sem, slot_sem, halo_send, halo_recv, denx_send, denx_recv, denz_send, denz_recv,
    x_send, x_recv, z_send, z_recv, x_token, z_token,
):
    span = nz // NCHUNK
    me, patch = lax.axis_index("exp"), lax.axis_index("patch")
    zpos, xpos = me // NX, me % NX
    barrier = pltpu.get_barrier_semaphore()

    def along_x(n):
        return (zpos * NX + (xpos + n) % NX, patch)

    def at_z(z):
        return (z * NX + xpos, patch)

    def remote(src, dst, ssem, rsem, target):
        return pltpu.make_async_remote_copy(
            src_ref=src, dst_ref=dst, send_sem=ssem, recv_sem=rsem, device_id=target, device_id_type=MESH
        )

    def signal(sem, target):
        pl.semaphore_signal(sem, inc=1, device_id=target, device_id_type=MESH)

    def halo(way):
        source, target = ((NROWS, 0), (PAD, PAD + NROWS))[way]
        return remote(
            buf.at[:, pl.ds(source, PAD), :],
            buf.at[:, pl.ds(target, PAD), :],
            halo_send.at[way],
            halo_recv.at[way],
            (me, patch + (1, -1)[way]),
        )

    def den_x(n):
        return remote(denx.at[0], denx.at[n], denx_send.at[n], denx_recv.at[n], along_x(n))

    def den_z(z, slot):
        return remote(denz.at[nz], denz.at[slot], denz_send.at[z], denz_recv.at[slot], at_z(z))

    def cells_x(n, g):
        rows = pl.ds(g * span, span)
        return remote(
            send.at[(xpos + n) % NX, rows], recv_x.at[n - 1, rows], x_send.at[n - 1, g], x_recv.at[n - 1, g], along_x(n)
        )

    def cells_z(z, slot):
        return remote(xsum.at[z], recv_z.at[slot], z_send.at[z], z_recv.at[slot], at_z(z))

    def others(action, start=0, stop=None):
        def one(z, carry):
            @pl.when(z != zpos)
            def _():
                action(z)

            return carry

        lax.fori_loop(start, nz if stop is None else stop, one, 0)

    def around(action):
        def one(d, carry):
            action((zpos + d) % nz)
            action((zpos + nz - d) % nz)
            return carry

        lax.fori_loop(1, nz // 2, one, 0)
        action((zpos + nz // 2) % nz)

    pairs = ((offs_hbm, offs), (cell_hbm, cell), (coef_hbm, coef), (wgt_hbm, wgt), (row_hbm, rowt), (col_hbm, colt))
    loads = [pltpu.make_async_copy(src, dst, load_sem.at[4 + k]) for k, (src, dst) in enumerate(pairs)]
    bands = [
        pltpu.make_async_copy(
            img_hbm.at[:, pl.ds(j * 128, 128)], buf.at[j, pl.ds(PAD, NROWS), :], load_sem.at[j]
        )
        for j in range(4)
    ]
    for copy in loads + bands:
        copy.start()

    upper, lower = patch > 0, patch < npatch - 1

    @pl.when(upper)
    def _():
        signal(barrier, (me, patch - 1))

    @pl.when(lower)
    def _():
        signal(barrier, (me, patch + 1))

    for n in (1, NX - 1):
        signal(barrier, along_x(n))
    for d in (1, nz - 1):
        signal(barrier, at_z((zpos + d) % nz))

    for copy in loads:
        copy.wait()
    build_weights(coef, rowt, colt, scaled, phigh, plow)

    lane = lanes(8)
    first = jnp.full((8, 128), NTILES, jnp.int32)
    last = jnp.full((8, 128), -1, jnp.int32)
    count = jnp.zeros((8, 128), F32)
    for k in range(NTILES):
        hit = lane == cell[0, k]
        count = count + jnp.where(hit, 1.0, 0.0)
        first = jnp.minimum(first, jnp.where(hit, k, NTILES))
        last = jnp.maximum(last, jnp.where(hit, k, -1))
    sub = lax.broadcasted_iota(jnp.int32, (8, 128), 0)
    slotv[...] = jnp.where(sub == 0, first, jnp.where(last > first, last, NTILES))
    slot_copy = pltpu.make_async_copy(slotv, slots, slot_sem)
    slot_copy.start()
    denx[0] = (count * wgt[0])[0:1]

    pl.semaphore_wait(barrier, jnp.where(upper, 1, 0) + jnp.where(lower, 1, 0) + 4)
    for copy in bands:
        copy.wait()

    @pl.when(lower)
    def _():
        halo(0).start()

    @pl.when(upper)
    def _():
        halo(1).start()

    for n in (1, NX - 1):
        signal(x_token, along_x(n))
    reach = 1
    rounds = []
    while reach < nz // 2:
        rounds.append(reach)
        reach *= 2

    def greet(r):
        for d in (rounds[r], nz - rounds[r]):
            signal(z_token.at[r], at_z((zpos + d) % nz))

    greet(0)

    @pl.when(jnp.logical_not(upper))
    def _():
        buf[:, 0:PAD, :] = jnp.zeros((4, PAD, 128), F32)

    @pl.when(jnp.logical_not(lower))
    def _():
        buf[:, PAD + NROWS : PAD + NROWS + PAD, :] = jnp.zeros((4, PAD, 128), F32)

    buf[:, PAD + NROWS + PAD :, :] = jnp.zeros((4, NG * ROWQ - NROWS - 2 * PAD, 128), F32)

    @pl.when(upper)
    def _():
        halo(0).wait_recv()

    @pl.when(lower)
    def _():
        halo(1).wait_recv()

    build_planes(buf, phi, plo)
    pl.semaphore_wait(x_token, 2)
    for n in range(1, NX):
        den_x(n).start()
    done = 0
    for r in range(1, len(rounds)):
        pl.semaphore_wait(z_token.at[r - 1], 2)
        greet(r)
        convolve(range(done, done + 4), phi, plo, phigh, plow, acc)
        done += 4
    convolve(range(done, NA), phi, plo, phigh, plow, acc)
    to_matched(acc, mat, wgt[0])
    cut_tiles(offs, mat, tiles)
    slot_copy.wait()

    def gather(depth, carry):
        for x in range(NX):
            place = depth * NX + x
            send[x, depth] = tiles[slots[0, place]] + tiles[slots[1, place]]
        return carry

    for g in range(NCHUNK):
        lax.fori_loop(g * span, (g + 1) * span, gather, 0)
        for n in (2, 1, 3):
            cells_x(n, g).start()

    pl.semaphore_wait(z_token.at[len(rounds) - 1], 2)
    for n in range(1, NX):
        den_x(n).wait_recv()
    denz[nz] = denx[0] + denx[1] + denx[2] + denx[3]
    others(lambda z: den_z(z, zpos).start())

    for g in range(NCHUNK):
        for n in range(1, NX):
            cells_x(n, g).wait_recv()
        rows = pl.ds(g * span, span)
        xsum[rows] = (send[xpos, rows] + recv_x[0, rows]) + (recv_x[1, rows] + recv_x[2, rows])
        others(lambda z: cells_z(z, zpos).start(), g * span, (g + 1) * span)

    around(lambda z: den_z(z, z).wait_recv())
    denz[zpos] = denz[nz]
    den = denz[0]
    for z in range(1, nz):
        den = den + denz[z]
    den = jnp.sum(jnp.where(lanes(1) == me, den, 0.0), axis=1, keepdims=True)
    out_ref[...] = xsum[zpos]

    def add(z):
        cells_z(z, z).wait_recv()
        out_ref[...] += recv_z[z]

    around(add)
    out_ref[...] = out_ref[...] / den

    @pl.when(lower)
    def _():
        halo(0).wait_send()

    @pl.when(upper)
    def _():
        halo(1).wait_send()

    for n in range(1, NX):
        den_x(n).wait_send()
        for g in range(NCHUNK):
            cells_x(n, g).wait_send()
    others(lambda z: den_z(z, zpos).wait_send())
    others(lambda z: cells_z(z, zpos).wait_send())


def per_device(nz, npatch, image, row_taps, col_taps, coefficients, exposure_weight, warp_offset, target_cell):
    hbm = pl.BlockSpec(memory_space=pltpu.HBM)
    vmem = pltpu.VMEM
    smem = pltpu.SMEM
    dma = pltpu.SemaphoreType.DMA
    rounds = max(1, (nz // 2 - 1).bit_length())
    out = pl.pallas_call(
        functools.partial(kernel, nz, npatch),
        out_shape=jax.ShapeDtypeStruct((TR, TW), F32),
        in_specs=[hbm] * 7,
        out_specs=pl.BlockSpec(memory_space=vmem),
        scratch_shapes=[
            smem((1, NTILES), jnp.int32),
            smem((1, NTILES), jnp.int32),
            smem((1, NB), F32),
            smem((1,), F32),
            vmem((NB, TAPS), F32),
            vmem((NB, TAPS), F32),
            vmem((4, NG * ROWQ, 128), F32),
            vmem((NB, TAPS), F32),
            vmem(((NKAP + 2) * 128, 128), BF16),
            vmem(((NKAP + 2) * 128, 128), BF16),
            vmem((ROWQ, NJ, NG, 128), F32),
            vmem((ROWQ, NJ, NG, 128), F32),
            vmem((NJ * NQ, 256), F32),
            vmem((6, NROWS, 128), F32),
            vmem((NTILES + 1, TR, TW), F32),
            vmem((8, 128), jnp.int32),
            smem((8, 128), jnp.int32),
            vmem((NX, 1, 128), F32),
            vmem((nz + 1, 1, 128), F32),
            vmem((NX, nz, TR, TW), F32),
            vmem((NX - 1, nz, TR, TW), F32),
            vmem((nz, TR, TW), F32),
            vmem((nz, TR, TW), F32),
            dma((10,)),
            dma,
            dma((2,)),
            dma((2,)),
            dma((NX,)),
            dma((NX,)),
            dma((nz,)),
            dma((nz,)),
            dma((NX - 1, NCHUNK)),
            dma((NX - 1, NCHUNK)),
            dma((nz,)),
            dma((nz,)),
            pltpu.SemaphoreType.REGULAR,
            pltpu.SemaphoreType.REGULAR((rounds,)),
        ],
        compiler_params=pltpu.CompilerParams(
            collective_id=0, has_side_effects=True, vmem_limit_bytes=60 * 2**20
        ),
    )(
        warp_offset.reshape(1, NTILES),
        target_cell.reshape(1, NTILES),
        coefficients,
        exposure_weight,
        row_taps,
        col_taps,
        image.reshape(NROWS, NCOLS),
    )
    return out[None, None]


def solution(mesh):
    nz = mesh.shape["exp"] // NX
    npatch = mesh.shape["patch"]
    return jax.shard_map(
        functools.partial(per_device, nz, npatch),
        mesh=mesh,
        in_specs=(
            P("exp", "patch", None),
            P(),
            P(),
            P("exp", None),
            P("exp"),
            P("exp", "patch", None),
            P("exp", "patch", None, None),
        ),
        out_specs=P("patch", "exp", None, None),
        check_vma=False,
    )
```

```python
import functools

import jax
import jax.numpy as jnp
from jax import lax
from jax.experimental import pallas as pl
from jax.experimental.pallas import tpu as pltpu
from jax.sharding import PartitionSpec as P

NB = 20
TAPS = 41
HALF = 20
NROWS = 128
NCOLS = 512
TR = 16
TW = 128
SHIFT = 8
NTILES = 32
NX = 4
PAD = 24
F32 = jnp.float32
BF16 = jnp.bfloat16
MESH = pl.DeviceIdType.MESH
ROWQ = 4
XB = 64
NJ = NCOLS // XB
NA = (ROWQ + TAPS + ROWQ - 2) // ROWQ
NKAP = NA * ROWQ
NQ = NROWS // ROWQ
NG = 48
EDGE = 16
EARLY, MID, LATE = 1, 5, 9
AHEAD = 2
BOUNDS = (0, 2, 5, 10, 16)


def chunk_bounds(nz):
    return tuple(sorted({0, nz} | {max(1, nz * step // 16) for step in BOUNDS[1:]}))


def lanes(rows):
    return lax.broadcasted_iota(jnp.int32, (rows, 128), 1)


def build_weights(coef_ref, row_ref, col_ref, scaled, phigh, plow):
    for b in range(NB):
        scaled[b : b + 1, :] = col_ref[b : b + 1, :] * coef_ref[0, b]
    tap = lax.broadcasted_iota(jnp.int32, (TAPS, 128), 0)
    place = lax.broadcasted_iota(jnp.int32, (TAPS, 128), 1)
    flip = jnp.where((XB - place % XB) % XB == tap, 1.0, 0.0).astype(F32)
    rowpat = jnp.dot(row_ref[...], flip, precision=lax.Precision.HIGHEST, preferred_element_type=F32)
    pats = lax.dot_general(
        scaled[...], rowpat, (((0,), (0,)), ((), ())), precision=lax.Precision.HIGHEST, preferred_element_type=F32
    )
    left = lanes(XB) < XB
    gap = lax.broadcasted_iota(jnp.int32, (128, 128), 0) - lanes(128) % XB
    keep = (gap >= 0) & (gap < TAPS)
    zero = jnp.zeros((XB, 128), F32)
    rings = [zero] * (ROWQ - 1)
    for i in range(TAPS):
        base = jnp.broadcast_to(pats[i : i + 1, :], (XB, 128))
        rings.append(pltpu.roll(base, 0, 1, stride=1, stride_axis=0))
    rings += [zero] * ROWQ
    for kappa in range(-2, NKAP):
        pair = jnp.where(left, rings[kappa + 3], rings[kappa + 2])
        band = jnp.where(keep, jnp.concatenate([pair, pair], axis=0), 0.0)
        high = band.astype(BF16)
        rows = slice((kappa + 2) * 128, (kappa + 3) * 128)
        phigh[rows, :] = high
        plow[rows, :] = (band - high.astype(F32)).astype(BF16)


def build_planes(groups, buf, phi, plo):
    lane = lanes(groups)
    zero = jnp.zeros((groups, 128), F32)
    for rho in range(ROWQ):
        cols = [buf[j, pl.ds(rho, groups, stride=ROWQ), :] for j in range(4)]
        padded = [zero] + cols + [zero]
        for j in range(4):
            even = jnp.where(lane < HALF, pltpu.roll(padded[j], HALF, 1), pltpu.roll(padded[j + 1], HALF, 1))
            odd = jnp.where(
                lane < XB + HALF, pltpu.roll(padded[j + 1], XB + HALF, 1), pltpu.roll(padded[j + 2], XB + HALF, 1)
            )
            for place, part in ((2 * j, even), (2 * j + 1, odd)):
                high = part.astype(BF16).astype(F32)
                phi[rho, place] = high
                plo[rho, place] = part - high


def products(a, start, rows, phi, plo, phigh, plow):
    def lhs(src):
        return jnp.concatenate(
            [
                jnp.concatenate([src[rho, j, start : start + rows, :].astype(BF16) for j in range(NJ)], axis=0)
                for rho in range(ROWQ)
            ],
            axis=1,
        )

    def rhs(src):
        return jnp.concatenate(
            [src[(a * ROWQ + 2) * 128 : (a * ROWQ + 6) * 128, :], src[a * ROWQ * 128 : (a * ROWQ + 4) * 128, :]], axis=1
        )

    def dot(x, y):
        return jnp.dot(x, y, preferred_element_type=F32)

    high, low = lhs(phi), lhs(plo)
    wide, fine = rhs(phigh), rhs(plow)
    return dot(high, wide) + dot(low, wide) + dot(high, fine)


def convolve(steps, phi, plo, phigh, plow, acc):
    for a in steps:
        part = products(a, a + 1, NQ, phi, plo, phigh, plow)
        if a == 0:
            acc[...] = part
        else:
            acc[...] += part


def add_edges(ehi, elo, phigh, plow, acc):
    reach = HALF // ROWQ
    tops = [products(a, a + 1, 8, ehi, elo, phigh, plow) for a in range(reach)]
    ends = [products(a, EDGE + a - 5, 8, ehi, elo, phigh, plow) for a in range(NA - reach, NA)]
    for parts, row in ((tops, 0), (ends, NQ - 8)):
        total = sum(parts[1:], parts[0])
        for j in range(NJ):
            acc[j * NQ + row : j * NQ + row + 8, :] += total[j * 8 : j * 8 + 8, :]


def to_matched(acc, mat, weight):
    left = lanes(NQ) < XB
    mat[0] = jnp.zeros((NROWS, 128), F32)
    mat[5] = jnp.zeros((NROWS, 128), F32)
    for j in range(4):
        for pair in range(2):
            cols = slice(pair * 128, pair * 128 + 128)
            even = acc[2 * j * NQ : (2 * j + 1) * NQ, cols] * weight
            odd = acc[(2 * j + 1) * NQ : (2 * j + 2) * NQ, cols] * weight
            mat[j + 1, pl.ds(2 * pair, NQ, stride=ROWQ), :] = jnp.where(left, even, pltpu.roll(odd, XB, 1))
            mat[j + 1, pl.ds(2 * pair + 1, NQ, stride=ROWQ), :] = jnp.where(left, pltpu.roll(even, XB, 1), odd)


def cut_tiles(offs_ref, mat, tiles):
    lane = lanes(TR)
    tiles[NTILES] = jnp.zeros((TR, 128), F32)
    for k in range(NTILES):
        t, q = k // 4, k % 4
        rows = slice(t * TR, t * TR + TR)
        off = offs_ref[0, k]
        side = jnp.where(off >= SHIFT, q + 2, q)
        turn = (128 + SHIFT - off) % 128
        own = pltpu.roll(mat[q + 1, rows, :], turn, 1)
        other = pltpu.roll(mat[side, rows, :], turn, 1)
        source = lane + (off - SHIFT)
        tiles[k] = jnp.where((source >= 0) & (source < 128), own, other)


def kernel(
    nz, npatch,
    offs_hbm, cell_hbm, coef_hbm, wgt_hbm, row_hbm, col_hbm, img_hbm, out_ref,
    offs, cell, coef, wgt, rowt, colt,
    buf, edge, scaled, phigh, plow, phi, plo, ehi, elo, acc, mat, tiles,
    slotv, slots, denx, denz, send, recv_x, xsum, recv_z,
    load_sem, slot_sem, halo_send, halo_recv, denx_send, denx_recv, denz_send, denz_recv,
    x_send, x_recv, z_send, z_recv, x_token, z_token,
):
    bounds = chunk_bounds(nz)
    me, patch = lax.axis_index("exp"), lax.axis_index("patch")
    zpos, xpos = me // NX, me % NX
    barrier = pltpu.get_barrier_semaphore()

    def along_x(n):
        return (zpos * NX + (xpos + n) % NX, patch)

    def at_z(z):
        return (z * NX + xpos, patch)

    def remote(src, dst, ssem, rsem, target):
        return pltpu.make_async_remote_copy(
            src_ref=src, dst_ref=dst, send_sem=ssem, recv_sem=rsem, device_id=target, device_id_type=MESH
        )

    def signal(sem, target):
        pl.semaphore_signal(sem, inc=1, device_id=target, device_id_type=MESH)

    def halo(way):
        source, target = ((NROWS, 0), (PAD, (EDGE + 8) * ROWQ))[way]
        return remote(
            buf.at[:, pl.ds(source, PAD), :],
            edge.at[:, pl.ds(target, PAD), :],
            halo_send.at[way],
            halo_recv.at[way],
            (me, patch + (1, -1)[way]),
        )

    def den_x(n):
        return remote(denx.at[0], denx.at[n], denx_send.at[n], denx_recv.at[n], along_x(n))

    def den_z(z, slot):
        return remote(denz.at[nz], denz.at[slot], denz_send.at[z], denz_recv.at[slot], at_z(z))

    def cells_x(n, g):
        rows = pl.ds(bounds[g], bounds[g + 1] - bounds[g])
        return remote(
            send.at[(xpos + n) % NX, rows], recv_x.at[n - 1, rows], x_send.at[n - 1, g], x_recv.at[n - 1, g], along_x(n)
        )

    def cells_z(z, slot):
        return remote(xsum.at[z], recv_z.at[slot], z_send.at[z], z_recv.at[slot], at_z(z))

    def others(action, start=0, stop=None):
        def one(z, carry):
            @pl.when(z != zpos)
            def _():
                action(z)

            return carry

        lax.fori_loop(start, nz if stop is None else stop, one, 0)

    def around(action):
        def one(d, carry):
            action((zpos + d) % nz)
            action((zpos + nz - d) % nz)
            return carry

        lax.fori_loop(1, nz // 2, one, 0)
        action((zpos + nz // 2) % nz)

    pairs = ((offs_hbm, offs), (cell_hbm, cell), (coef_hbm, coef), (wgt_hbm, wgt), (row_hbm, rowt), (col_hbm, colt))
    loads = [pltpu.make_async_copy(src, dst, load_sem.at[4 + k]) for k, (src, dst) in enumerate(pairs)]
    bands = [
        pltpu.make_async_copy(
            img_hbm.at[:, pl.ds(j * 128, 128)], buf.at[j, pl.ds(PAD, NROWS), :], load_sem.at[j]
        )
        for j in range(4)
    ]
    for copy in loads + bands:
        copy.start()

    upper, lower = patch > 0, patch < npatch - 1

    @pl.when(upper)
    def _():
        signal(barrier, (me, patch - 1))

    @pl.when(lower)
    def _():
        signal(barrier, (me, patch + 1))

    for n in (1, NX - 1):
        signal(barrier, along_x(n))
    for d in (1, nz - 1):
        signal(barrier, at_z((zpos + d) % nz))

    for copy in loads:
        copy.wait()
    build_weights(coef, rowt, colt, scaled, phigh, plow)

    lane = lanes(8)
    first = jnp.full((8, 128), NTILES, jnp.int32)
    last = jnp.full((8, 128), -1, jnp.int32)
    count = jnp.zeros((8, 128), F32)
    for k in range(NTILES):
        hit = lane == cell[0, k]
        count = count + jnp.where(hit, 1.0, 0.0)
        first = jnp.minimum(first, jnp.where(hit, k, NTILES))
        last = jnp.maximum(last, jnp.where(hit, k, -1))
    sub = lax.broadcasted_iota(jnp.int32, (8, 128), 0)
    slotv[...] = jnp.where(sub == 0, first, jnp.where(last > first, last, NTILES))
    slot_copy = pltpu.make_async_copy(slotv, slots, slot_sem)
    slot_copy.start()
    denx[0] = (count * wgt[0])[0:1]

    buf[:, 0:PAD, :] = jnp.zeros((4, PAD, 128), F32)
    buf[:, PAD + NROWS :, :] = jnp.zeros((4, NG * ROWQ - NROWS - PAD, 128), F32)
    top, end = slice(0, PAD), slice((EDGE + 8) * ROWQ, (EDGE + 8) * ROWQ + PAD)
    edge[:, PAD : end.start, :] = jnp.zeros((4, end.start - PAD, 128), F32)
    edge[:, end.stop :, :] = jnp.zeros((4, 2 * EDGE * ROWQ - end.stop, 128), F32)

    @pl.when(jnp.logical_not(upper))
    def _():
        edge[:, top, :] = jnp.zeros((4, PAD, 128), F32)

    @pl.when(jnp.logical_not(lower))
    def _():
        edge[:, end, :] = jnp.zeros((4, PAD, 128), F32)

    for copy in bands:
        copy.wait()
    build_planes(NG, buf, phi, plo)
    convolve(range(0, EARLY), phi, plo, phigh, plow, acc)

    pl.semaphore_wait(barrier, jnp.where(upper, 1, 0) + jnp.where(lower, 1, 0) + 4)

    @pl.when(lower)
    def _():
        halo(0).start()

    @pl.when(upper)
    def _():
        halo(1).start()

    for n in (1, NX - 1):
        signal(x_token, along_x(n))
    rounds = [1 << r for r in range(max(1, (nz // 2 - 1).bit_length()))]

    def greet(r):
        for d in (rounds[r], nz - rounds[r]):
            signal(z_token.at[r], at_z((zpos + d) % nz))

    greet(0)
    stops = [EARLY, MID, LATE][: len(rounds)] + [NA]
    for r in range(len(rounds)):
        convolve(range(stops[r], stops[r + 1]), phi, plo, phigh, plow, acc)
        if r + 1 < len(rounds):
            pl.semaphore_wait(z_token.at[r], 2)
            greet(r + 1)
        if r == 0:
            pl.semaphore_wait(x_token, 2)
            for n in range(1, NX):
                den_x(n).start()

    @pl.when(upper)
    def _():
        halo(0).wait_recv()

    @pl.when(lower)
    def _():
        halo(1).wait_recv()

    build_planes(2 * EDGE, edge, ehi, elo)
    add_edges(ehi, elo, phigh, plow, acc)
    to_matched(acc, mat, wgt[0])
    cut_tiles(offs, mat, tiles)
    slot_copy.wait()

    groups = len(bounds) - 1

    def send_x(g):
        for depth in range(bounds[g], bounds[g + 1]):
            for x in range(NX):
                place = depth * NX + x
                send[x, depth] = tiles[slots[0, place]] + tiles[slots[1, place]]
        for n in (2, 1, 3):
            cells_x(n, g).start()

    for g in range(min(AHEAD, groups)):
        send_x(g)
    pl.semaphore_wait(z_token.at[len(rounds) - 1], 2)
    for n in range(1, NX):
        den_x(n).wait_recv()
    denz[nz] = denx[0] + denx[1] + denx[2] + denx[3]
    others(lambda z: den_z(z, zpos).start())

    for g in range(groups):
        for n in range(1, NX):
            cells_x(n, g).wait_recv()
        rows = pl.ds(bounds[g], bounds[g + 1] - bounds[g])
        xsum[rows] = (send[xpos, rows] + recv_x[0, rows]) + (recv_x[1, rows] + recv_x[2, rows])
        others(lambda z: cells_z(z, zpos).start(), bounds[g], bounds[g + 1])
        if g + AHEAD < groups:
            send_x(g + AHEAD)

    around(lambda z: den_z(z, z).wait_recv())
    denz[zpos] = denz[nz]
    den = denz[0]
    for z in range(1, nz):
        den = den + denz[z]
    den = jnp.sum(jnp.where(lanes(1) == me, den, 0.0), axis=1, keepdims=True)
    out_ref[...] = xsum[zpos]

    def add(z):
        cells_z(z, z).wait_recv()
        out_ref[...] += recv_z[z]

    around(add)
    out_ref[...] = out_ref[...] / den

    @pl.when(lower)
    def _():
        halo(0).wait_send()

    @pl.when(upper)
    def _():
        halo(1).wait_send()

    for n in range(1, NX):
        den_x(n).wait_send()
        for g in range(len(bounds) - 1):
            cells_x(n, g).wait_send()
    others(lambda z: den_z(z, zpos).wait_send())
    others(lambda z: cells_z(z, zpos).wait_send())


def per_device(nz, npatch, image, row_taps, col_taps, coefficients, exposure_weight, warp_offset, target_cell):
    hbm = pl.BlockSpec(memory_space=pltpu.HBM)
    vmem = pltpu.VMEM
    smem = pltpu.SMEM
    dma = pltpu.SemaphoreType.DMA
    rounds = max(1, (nz // 2 - 1).bit_length())
    out = pl.pallas_call(
        functools.partial(kernel, nz, npatch),
        out_shape=jax.ShapeDtypeStruct((TR, TW), F32),
        in_specs=[hbm] * 7,
        out_specs=pl.BlockSpec(memory_space=vmem),
        scratch_shapes=[
            smem((1, NTILES), jnp.int32),
            smem((1, NTILES), jnp.int32),
            smem((1, NB), F32),
            smem((1,), F32),
            vmem((NB, TAPS), F32),
            vmem((NB, TAPS), F32),
            vmem((4, NG * ROWQ, 128), F32),
            vmem((4, 2 * EDGE * ROWQ, 128), F32),
            vmem((NB, TAPS), F32),
            vmem(((NKAP + 2) * 128, 128), BF16),
            vmem(((NKAP + 2) * 128, 128), BF16),
            vmem((ROWQ, NJ, NG, 128), F32),
            vmem((ROWQ, NJ, NG, 128), F32),
            vmem((ROWQ, NJ, 2 * EDGE, 128), F32),
            vmem((ROWQ, NJ, 2 * EDGE, 128), F32),
            vmem((NJ * NQ, 256), F32),
            vmem((6, NROWS, 128), F32),
            vmem((NTILES + 1, TR, TW), F32),
            vmem((8, 128), jnp.int32),
            smem((8, 128), jnp.int32),
            vmem((NX, 1, 128), F32),
            vmem((nz + 1, 1, 128), F32),
            vmem((NX, nz, TR, TW), F32),
            vmem((NX - 1, nz, TR, TW), F32),
            vmem((nz, TR, TW), F32),
            vmem((nz, TR, TW), F32),
            dma((10,)),
            dma,
            dma((2,)),
            dma((2,)),
            dma((NX,)),
            dma((NX,)),
            dma((nz,)),
            dma((nz,)),
            dma((NX - 1, len(chunk_bounds(nz)) - 1)),
            dma((NX - 1, len(chunk_bounds(nz)) - 1)),
            dma((nz,)),
            dma((nz,)),
            pltpu.SemaphoreType.REGULAR,
            pltpu.SemaphoreType.REGULAR((rounds,)),
        ],
        compiler_params=pltpu.CompilerParams(
            collective_id=0, has_side_effects=True, vmem_limit_bytes=48 * 2**20
        ),
    )(
        *(
            part if part.size == 1 else pltpu.with_memory_space_constraint(part, pltpu.HBM)
            for part in (
                warp_offset.reshape(1, NTILES),
                target_cell.reshape(1, NTILES),
                coefficients,
                exposure_weight,
                row_taps,
                col_taps,
                image.reshape(NROWS, NCOLS),
            )
        )
    )
    return out[None, None]


def solution(mesh):
    nz = mesh.shape["exp"] // NX
    npatch = mesh.shape["patch"]
    return jax.shard_map(
        functools.partial(per_device, nz, npatch),
        mesh=mesh,
        in_specs=(
            P("exp", "patch", None),
            P(),
            P(),
            P("exp", None),
            P("exp"),
            P("exp", "patch", None),
            P("exp", "patch", None, None),
        ),
        out_specs=P("patch", "exp", None, None),
        check_vma=False,
    )
```

```python
import functools

import jax
import jax.numpy as jnp
from jax import lax
from jax.experimental import pallas as pl
from jax.experimental.pallas import tpu as pltpu
from jax.sharding import PartitionSpec as P

NB = 20
TAPS = 41
HALF = 20
NROWS = 128
NCOLS = 512
TR = 16
TW = 128
SHIFT = 8
NTILES = 32
NX = 4
PAD = 24
F32 = jnp.float32
BF16 = jnp.bfloat16
MESH = pl.DeviceIdType.MESH
ROWQ = 4
XB = 64
NJ = NCOLS // XB
NA = (ROWQ + TAPS + ROWQ - 2) // ROWQ
NKAP = NA * ROWQ
NQ = NROWS // ROWQ
NG = 48
EDGE = 16
MID, LATE = 5, 11
AHEAD = 9
BOUNDS = (0, 2, 5, 10, 16)


def chunk_bounds(nz):
    return tuple(sorted({0, nz} | {max(1, nz * step // 16) for step in BOUNDS[1:]}))


def lanes(rows):
    return lax.broadcasted_iota(jnp.int32, (rows, 128), 1)


def build_weights(coef_ref, row_ref, col_ref, scaled, phigh, plow):
    for b in range(NB):
        scaled[b : b + 1, :] = col_ref[b : b + 1, :] * coef_ref[0, b]
    tap = lax.broadcasted_iota(jnp.int32, (TAPS, 128), 0)
    place = lax.broadcasted_iota(jnp.int32, (TAPS, 128), 1)
    flip = jnp.where((XB - place % XB) % XB == tap, 1.0, 0.0).astype(F32)
    rowpat = jnp.dot(row_ref[...], flip, precision=lax.Precision.HIGHEST, preferred_element_type=F32)
    pats = lax.dot_general(
        scaled[...], rowpat, (((0,), (0,)), ((), ())), precision=lax.Precision.HIGHEST, preferred_element_type=F32
    )
    left = lanes(XB) < XB
    gap = lax.broadcasted_iota(jnp.int32, (128, 128), 0) - lanes(128) % XB
    keep = (gap >= 0) & (gap < TAPS)
    zero = jnp.zeros((XB, 128), F32)
    rings = [zero] * (ROWQ - 1)
    for i in range(TAPS):
        base = jnp.broadcast_to(pats[i : i + 1, :], (XB, 128))
        rings.append(pltpu.roll(base, 0, 1, stride=1, stride_axis=0))
    rings += [zero] * ROWQ
    for kappa in range(-2, NKAP):
        pair = jnp.where(left, rings[kappa + 3], rings[kappa + 2])
        band = jnp.where(keep, jnp.concatenate([pair, pair], axis=0), 0.0)
        high = band.astype(BF16)
        rows = slice((kappa + 2) * 128, (kappa + 3) * 128)
        phigh[rows, :] = high
        plow[rows, :] = (band - high.astype(F32)).astype(BF16)


def build_planes(groups, base, buf, phi, plo):
    lane = lanes(groups)
    zero = jnp.zeros((groups, 128), F32)
    for rho in range(ROWQ):
        cols = [buf[j, pl.ds(rho, groups, stride=ROWQ), :] for j in range(4)]
        padded = [zero] + cols + [zero]
        for j in range(4):
            even = jnp.where(lane < HALF, pltpu.roll(padded[j], HALF, 1), pltpu.roll(padded[j + 1], HALF, 1))
            odd = jnp.where(
                lane < XB + HALF, pltpu.roll(padded[j + 1], XB + HALF, 1), pltpu.roll(padded[j + 2], XB + HALF, 1)
            )
            for place, part in ((2 * j, even), (2 * j + 1, odd)):
                high = part.astype(BF16).astype(F32)
                phi[rho, place, base : base + groups, :] = high
                plo[rho, place, base : base + groups, :] = part - high


def products(a, start, rows, phi, plo, phigh, plow):
    def lhs(src):
        return jnp.concatenate(
            [
                jnp.concatenate([src[rho, j, start : start + rows, :].astype(BF16) for j in range(NJ)], axis=0)
                for rho in range(ROWQ)
            ],
            axis=1,
        )

    def rhs(src):
        return jnp.concatenate(
            [src[(a * ROWQ + 2) * 128 : (a * ROWQ + 6) * 128, :], src[a * ROWQ * 128 : (a * ROWQ + 4) * 128, :]], axis=1
        )

    def dot(x, y):
        return jnp.dot(x, y, preferred_element_type=F32)

    high, low = lhs(phi), lhs(plo)
    both = dot(jnp.concatenate([high, low], axis=0), rhs(phigh))
    return both[: NJ * rows] + both[NJ * rows :] + dot(high, rhs(plow))


def convolve(steps, phi, plo, phigh, plow, acc):
    for a in steps:
        part = products(a, a + 1, NQ, phi, plo, phigh, plow)
        if a == 0:
            acc[...] = part
        else:
            acc[...] += part


def add_edges(ehi, elo, phigh, plow, acc):
    reach = HALF // ROWQ
    tops = [products(a, EDGE + a + 1, 8, ehi, elo, phigh, plow) for a in range(reach)]
    ends = [products(a, a - 5, 8, ehi, elo, phigh, plow) for a in range(NA - reach, NA)]
    for parts, row in ((tops, 0), (ends, NQ - 8)):
        total = sum(parts[1:], parts[0])
        for j in range(NJ):
            acc[j * NQ + row : j * NQ + row + 8, :] += total[j * 8 : j * 8 + 8, :]


def to_matched(acc, mat, weight):
    left = lanes(NQ) < XB
    mat[0] = jnp.zeros((NROWS, 128), F32)
    mat[5] = jnp.zeros((NROWS, 128), F32)
    for j in range(4):
        for pair in range(2):
            cols = slice(pair * 128, pair * 128 + 128)
            even = acc[2 * j * NQ : (2 * j + 1) * NQ, cols] * weight
            odd = acc[(2 * j + 1) * NQ : (2 * j + 2) * NQ, cols] * weight
            mat[j + 1, pl.ds(2 * pair, NQ, stride=ROWQ), :] = jnp.where(left, even, pltpu.roll(odd, XB, 1))
            mat[j + 1, pl.ds(2 * pair + 1, NQ, stride=ROWQ), :] = jnp.where(left, pltpu.roll(even, XB, 1), odd)


def cut_tiles(offs_ref, mat, tiles):
    lane = lanes(TR)
    tiles[NTILES] = jnp.zeros((TR, 128), F32)
    for k in range(NTILES):
        t, q = k // 4, k % 4
        rows = slice(t * TR, t * TR + TR)
        off = offs_ref[0, k]
        side = jnp.where(off >= SHIFT, q + 2, q)
        turn = (128 + SHIFT - off) % 128
        own = pltpu.roll(mat[q + 1, rows, :], turn, 1)
        other = pltpu.roll(mat[side, rows, :], turn, 1)
        source = lane + (off - SHIFT)
        tiles[k] = jnp.where((source >= 0) & (source < 128), own, other)


def kernel(
    nz, npatch,
    offs_hbm, cell_hbm, coef_hbm, wgt_hbm, row_hbm, col_hbm, img_hbm, out_ref,
    offs, cell, coef, wgt, rowt, colt,
    buf, edge, scaled, phigh, plow, phi, plo, ehi, elo, acc, mat, tiles,
    slotv, slots, denx, denz, send, recv_x, xsum, recv_z,
    load_sem, slot_sem, halo_send, halo_recv, denx_send, denx_recv, denz_send, denz_recv,
    x_send, x_recv, z_send, z_recv, x_token, z_token,
):
    bounds = chunk_bounds(nz)
    me, patch = lax.axis_index("exp"), lax.axis_index("patch")
    zpos, xpos = me // NX, me % NX
    barrier = pltpu.get_barrier_semaphore()

    def along_x(n):
        return (zpos * NX + (xpos + n) % NX, patch)

    def at_z(z):
        return (z * NX + xpos, patch)

    def remote(src, dst, ssem, rsem, target):
        return pltpu.make_async_remote_copy(
            src_ref=src, dst_ref=dst, send_sem=ssem, recv_sem=rsem, device_id=target, device_id_type=MESH
        )

    def signal(sem, target):
        pl.semaphore_signal(sem, inc=1, device_id=target, device_id_type=MESH)

    def halo(way):
        source, target = ((NROWS, 8 * ROWQ), (PAD, 0))[way]
        return remote(
            buf.at[:, pl.ds(source, PAD), :],
            edge.at[:, pl.ds(target, PAD), :],
            halo_send.at[way],
            halo_recv.at[way],
            (me, patch + (1, -1)[way]),
        )

    def den_x(n):
        return remote(denx.at[0], denx.at[n], denx_send.at[n], denx_recv.at[n], along_x(n))

    def den_z(z, slot):
        return remote(denz.at[nz], denz.at[slot], denz_send.at[z], denz_recv.at[slot], at_z(z))

    def cells_x(n, g):
        rows = pl.ds(bounds[g], bounds[g + 1] - bounds[g])
        return remote(
            send.at[(xpos + n) % NX, rows], recv_x.at[n - 1, rows], x_send.at[n - 1, g], x_recv.at[n - 1, g], along_x(n)
        )

    def cells_z(z, slot):
        return remote(xsum.at[z], recv_z.at[slot], z_send.at[z], z_recv.at[slot], at_z(z))

    def others(action, start=0, stop=None):
        def one(z, carry):
            @pl.when(z != zpos)
            def _():
                action(z)

            return carry

        lax.fori_loop(start, nz if stop is None else stop, one, 0)

    def around(action):
        def one(d, carry):
            action((zpos + d) % nz)
            action((zpos + nz - d) % nz)
            return carry

        lax.fori_loop(1, nz // 2, one, 0)
        action((zpos + nz // 2) % nz)

    pairs = ((offs_hbm, offs), (cell_hbm, cell), (coef_hbm, coef), (wgt_hbm, wgt), (row_hbm, rowt), (col_hbm, colt))
    loads = [pltpu.make_async_copy(src, dst, load_sem.at[4 + k]) for k, (src, dst) in enumerate(pairs)]
    bands = [
        pltpu.make_async_copy(
            img_hbm.at[:, pl.ds(j * 128, 128)], buf.at[j, pl.ds(PAD, NROWS), :], load_sem.at[j]
        )
        for j in range(4)
    ]
    for copy in loads + bands:
        copy.start()

    upper, lower = patch > 0, patch < npatch - 1

    @pl.when(upper)
    def _():
        signal(barrier, (me, patch - 1))

    @pl.when(lower)
    def _():
        signal(barrier, (me, patch + 1))

    for n in (1, NX - 1):
        signal(barrier, along_x(n))
    for d in (1, nz - 1):
        signal(barrier, at_z((zpos + d) % nz))

    for copy in loads:
        copy.wait()
    build_weights(coef, rowt, colt, scaled, phigh, plow)

    for copy in bands:
        copy.wait()
    pl.semaphore_wait(barrier, jnp.where(upper, 1, 0) + jnp.where(lower, 1, 0) + 4)

    @pl.when(lower)
    def _():
        halo(0).start()

    @pl.when(upper)
    def _():
        halo(1).start()

    for n in (1, NX - 1):
        signal(x_token, along_x(n))
    rounds = [1 << r for r in range(max(1, (nz // 2 - 1).bit_length()))]

    def greet(r):
        for d in (rounds[r], nz - rounds[r]):
            signal(z_token.at[r], at_z((zpos + d) % nz))

    greet(0)
    buf[:, 0:PAD, :] = jnp.zeros((4, PAD, 128), F32)
    buf[:, PAD + NROWS :, :] = jnp.zeros((4, NG * ROWQ - NROWS - PAD, 128), F32)
    gap = jnp.zeros((4, 8, 128), F32)
    edge[:, PAD : PAD + 8, :] = gap
    edge[:, EDGE * ROWQ - 8 :, :] = gap
    for plane in (ehi, elo):
        plane[:, :, 0:8, :] = jnp.zeros((ROWQ, NJ, 8, 128), F32)
        plane[:, :, EDGE + 8 :, :] = jnp.zeros((ROWQ, NJ, 8, 128), F32)

    @pl.when(jnp.logical_not(upper))
    def _():
        edge[:, 8 * ROWQ : 8 * ROWQ + PAD, :] = jnp.zeros((4, PAD, 128), F32)

    @pl.when(jnp.logical_not(lower))
    def _():
        edge[:, 0:PAD, :] = jnp.zeros((4, PAD, 128), F32)

    build_planes(NG, 0, buf, phi, plo)
    lane = lanes(8)
    first = jnp.full((8, 128), NTILES, jnp.int32)
    last = jnp.full((8, 128), -1, jnp.int32)
    count = jnp.zeros((8, 128), F32)
    for k in range(NTILES):
        hit = lane == cell[0, k]
        count = count + jnp.where(hit, 1.0, 0.0)
        first = jnp.minimum(first, jnp.where(hit, k, NTILES))
        last = jnp.maximum(last, jnp.where(hit, k, -1))
    sub = lax.broadcasted_iota(jnp.int32, (8, 128), 0)
    slotv[...] = jnp.where(sub == 0, first, jnp.where(last > first, last, NTILES))
    slot_copy = pltpu.make_async_copy(slotv, slots, slot_sem)
    slot_copy.start()
    denx[0] = (count * wgt[0])[0:1]

    stops = [0, MID, LATE][: len(rounds)] + [NA]
    for r in range(len(rounds)):
        convolve(range(stops[r], stops[r + 1]), phi, plo, phigh, plow, acc)
        if r + 1 < len(rounds):
            pl.semaphore_wait(z_token.at[r], 2)
            greet(r + 1)
        if r == 0:
            pl.semaphore_wait(x_token, 2)
            for n in range(1, NX):
                den_x(n).start()

    @pl.when(upper)
    def _():
        halo(0).wait_recv()

    @pl.when(lower)
    def _():
        halo(1).wait_recv()

    build_planes(EDGE, 8, edge, ehi, elo)
    add_edges(ehi, elo, phigh, plow, acc)
    to_matched(acc, mat, wgt[0])
    cut_tiles(offs, mat, tiles)
    slot_copy.wait()

    groups = len(bounds) - 1

    def send_x(g):
        for depth in range(bounds[g], bounds[g + 1]):
            for x in range(NX):
                place = depth * NX + x
                send[x, depth] = tiles[slots[0, place]] + tiles[slots[1, place]]
        for n in (2, 1, 3):
            cells_x(n, g).start()

    for g in range(min(AHEAD, groups)):
        send_x(g)
    pl.semaphore_wait(z_token.at[len(rounds) - 1], 2)
    for n in range(1, NX):
        den_x(n).wait_recv()
    denz[nz] = denx[0] + denx[1] + denx[2] + denx[3]
    others(lambda z: den_z(z, zpos).start())

    for g in range(groups):
        for n in range(1, NX):
            cells_x(n, g).wait_recv()
        rows = pl.ds(bounds[g], bounds[g + 1] - bounds[g])
        xsum[rows] = (send[xpos, rows] + recv_x[0, rows]) + (recv_x[1, rows] + recv_x[2, rows])
        others(lambda z: cells_z(z, zpos).start(), bounds[g], bounds[g + 1])
        if g + AHEAD < groups:
            send_x(g + AHEAD)

    around(lambda z: den_z(z, z).wait_recv())
    denz[zpos] = denz[nz]
    den = denz[0]
    for z in range(1, nz):
        den = den + denz[z]
    den = jnp.sum(jnp.where(lanes(1) == me, den, 0.0), axis=1, keepdims=True)
    out_ref[...] = xsum[zpos]

    def add(z):
        cells_z(z, z).wait_recv()
        out_ref[...] += recv_z[z]

    around(add)
    out_ref[...] = out_ref[...] / den

    @pl.when(lower)
    def _():
        halo(0).wait_send()

    @pl.when(upper)
    def _():
        halo(1).wait_send()

    for n in range(1, NX):
        den_x(n).wait_send()
        for g in range(len(bounds) - 1):
            cells_x(n, g).wait_send()
    others(lambda z: den_z(z, zpos).wait_send())
    others(lambda z: cells_z(z, zpos).wait_send())


def per_device(nz, npatch, image, row_taps, col_taps, coefficients, exposure_weight, warp_offset, target_cell):
    hbm = pl.BlockSpec(memory_space=pltpu.HBM)
    vmem = pltpu.VMEM
    smem = pltpu.SMEM
    dma = pltpu.SemaphoreType.DMA
    rounds = max(1, (nz // 2 - 1).bit_length())
    out = pl.pallas_call(
        functools.partial(kernel, nz, npatch),
        out_shape=jax.ShapeDtypeStruct((TR, TW), F32),
        in_specs=[hbm] * 7,
        out_specs=pl.BlockSpec(memory_space=vmem),
        scratch_shapes=[
            smem((1, NTILES), jnp.int32),
            smem((1, NTILES), jnp.int32),
            smem((1, NB), F32),
            smem((1,), F32),
            vmem((NB, TAPS), F32),
            vmem((NB, TAPS), F32),
            vmem((4, NG * ROWQ, 128), F32),
            vmem((4, EDGE * ROWQ, 128), F32),
            vmem((NB, TAPS), F32),
            vmem(((NKAP + 2) * 128, 128), BF16),
            vmem(((NKAP + 2) * 128, 128), BF16),
            vmem((ROWQ, NJ, NG, 128), F32),
            vmem((ROWQ, NJ, NG, 128), F32),
            vmem((ROWQ, NJ, 2 * EDGE, 128), F32),
            vmem((ROWQ, NJ, 2 * EDGE, 128), F32),
            vmem((NJ * NQ, 256), F32),
            vmem((6, NROWS, 128), F32),
            vmem((NTILES + 1, TR, TW), F32),
            vmem((8, 128), jnp.int32),
            smem((8, 128), jnp.int32),
            vmem((NX, 1, 128), F32),
            vmem((nz + 1, 1, 128), F32),
            vmem((NX, nz, TR, TW), F32),
            vmem((NX - 1, nz, TR, TW), F32),
            vmem((nz, TR, TW), F32),
            vmem((nz, TR, TW), F32),
            dma((10,)),
            dma,
            dma((2,)),
            dma((2,)),
            dma((NX,)),
            dma((NX,)),
            dma((nz,)),
            dma((nz,)),
            dma((NX - 1, len(chunk_bounds(nz)) - 1)),
            dma((NX - 1, len(chunk_bounds(nz)) - 1)),
            dma((nz,)),
            dma((nz,)),
            pltpu.SemaphoreType.REGULAR,
            pltpu.SemaphoreType.REGULAR((rounds,)),
        ],
        compiler_params=pltpu.CompilerParams(
            collective_id=0, has_side_effects=True, vmem_limit_bytes=48 * 2**20
        ),
    )(
        *(
            part if part.size == 1 else pltpu.with_memory_space_constraint(part, pltpu.HBM)
            for part in (
                warp_offset.reshape(1, NTILES),
                target_cell.reshape(1, NTILES),
                coefficients,
                exposure_weight,
                row_taps,
                col_taps,
                image.reshape(NROWS, NCOLS),
            )
        )
    )
    return out[None, None]


def solution(mesh):
    nz = mesh.shape["exp"] // NX
    npatch = mesh.shape["patch"]
    return jax.shard_map(
        functools.partial(per_device, nz, npatch),
        mesh=mesh,
        in_specs=(
            P("exp", "patch", None),
            P(),
            P(),
            P("exp", None),
            P("exp"),
            P("exp", "patch", None),
            P("exp", "patch", None, None),
        ),
        out_specs=P("patch", "exp", None, None),
        check_vma=False,
    )
```

```python
import functools

import jax
import jax.numpy as jnp
from jax import lax
from jax.experimental import pallas as pl
from jax.experimental.pallas import tpu as pltpu
from jax.sharding import PartitionSpec as P

NB = 20
TAPS = 41
HALF = 20
NROWS = 128
NCOLS = 512
TR = 16
TW = 128
SHIFT = 8
NTILES = 32
NX = 4
PAD = 24
F32 = jnp.float32
BF16 = jnp.bfloat16
MESH = pl.DeviceIdType.MESH
ROWQ = 4
XB = 64
NJ = NCOLS // XB
NA = (ROWQ + TAPS + ROWQ - 2) // ROWQ
NKAP = NA * ROWQ
NQ = NROWS // ROWQ
NG = 48
EDGE = 16
MID = 5
RELAY = (1, 4, 1)
AHEAD = 9
BOUNDS = (0, 1, 2, 4, 6, 8, 10, 12, 14, 16)


def chunk_bounds(nz):
    return tuple(sorted({0, nz} | {max(1, nz * step // 16) for step in BOUNDS[1:]}))


def lanes(rows):
    return lax.broadcasted_iota(jnp.int32, (rows, 128), 1)


def build_weights(coef_ref, row_ref, col_ref, scaled, phigh, plow):
    for b in range(NB):
        scaled[b : b + 1, :] = col_ref[b : b + 1, :] * coef_ref[0, b]
    tap = lax.broadcasted_iota(jnp.int32, (TAPS, 128), 0)
    place = lax.broadcasted_iota(jnp.int32, (TAPS, 128), 1)
    flip = jnp.where((XB - place % XB) % XB == tap, 1.0, 0.0).astype(F32)
    rowpat = jnp.dot(row_ref[...], flip, precision=lax.Precision.HIGHEST, preferred_element_type=F32)
    pats = lax.dot_general(
        scaled[...], rowpat, (((0,), (0,)), ((), ())), precision=lax.Precision.HIGHEST, preferred_element_type=F32
    )
    left = lanes(XB) < XB
    gap = lax.broadcasted_iota(jnp.int32, (128, 128), 0) - lanes(128) % XB
    keep = (gap >= 0) & (gap < TAPS)
    zero = jnp.zeros((XB, 128), F32)
    rings = [zero] * (ROWQ - 1)
    for i in range(TAPS):
        base = jnp.broadcast_to(pats[i : i + 1, :], (XB, 128))
        rings.append(pltpu.roll(base, 0, 1, stride=1, stride_axis=0))
    rings += [zero] * ROWQ
    for kappa in range(-2, NKAP):
        pair = jnp.where(left, rings[kappa + 3], rings[kappa + 2])
        band = jnp.where(keep, jnp.concatenate([pair, pair], axis=0), 0.0)
        high = band.astype(BF16)
        rows = slice((kappa + 2) * 128, (kappa + 3) * 128)
        phigh[rows, :] = high
        plow[rows, :] = (band - high.astype(F32)).astype(BF16)


def build_planes(groups, base, buf, phi, plo):
    lane = lanes(groups)
    zero = jnp.zeros((groups, 128), F32)
    rows = slice(base, base + groups)
    for rho in range(ROWQ):
        cols = [buf[j, pl.ds(rho, groups, stride=ROWQ), :] for j in range(4)]
        near = [zero] + [pltpu.roll(part, HALF, 1) for part in cols]
        far = [pltpu.roll(part, XB + HALF, 1) for part in cols] + [zero]
        for j in range(4):
            even = jnp.where(lane < HALF, near[j], near[j + 1])
            odd = jnp.where(lane < XB + HALF, far[j], far[j + 1])
            for place, part in ((2 * j, even), (2 * j + 1, odd)):
                high = part.astype(BF16).astype(F32)
                phi[rho, place, rows, :] = high
                plo[rho, place, rows, :] = part - high


def products(a, start, rows, phi, plo, phigh, plow):
    def lhs(src):
        return jnp.concatenate(
            [
                jnp.concatenate([src[rho, j, start : start + rows, :].astype(BF16) for j in range(NJ)], axis=0)
                for rho in range(ROWQ)
            ],
            axis=1,
        )

    def rhs(src):
        return jnp.concatenate(
            [src[(a * ROWQ + 2) * 128 : (a * ROWQ + 6) * 128, :], src[a * ROWQ * 128 : (a * ROWQ + 4) * 128, :]], axis=1
        )

    def dot(x, y):
        return jnp.dot(x, y, preferred_element_type=F32)

    high, low = lhs(phi), lhs(plo)
    both = dot(jnp.concatenate([high, low], axis=0), rhs(phigh))
    return both[: NJ * rows] + both[NJ * rows :] + dot(high, rhs(plow))


def convolve(steps, phi, plo, phigh, plow, acc):
    for a in steps:
        part = products(a, a + 3, NQ, phi, plo, phigh, plow)
        if a == 0:
            acc[...] = part
        else:
            acc[...] += part


def add_edges(ehi, elo, phigh, plow, acc):
    reach = HALF // ROWQ
    tops = [products(a, EDGE + a + 1, 8, ehi, elo, phigh, plow) for a in range(reach)]
    ends = [products(a, a - 5, 8, ehi, elo, phigh, plow) for a in range(NA - reach, NA)]
    for parts, row in ((tops, 0), (ends, NQ - 8)):
        total = sum(parts[1:], parts[0])
        for j in range(NJ):
            acc[j * NQ + row : j * NQ + row + 8, :] += total[j * 8 : j * 8 + 8, :]


def to_matched(acc, mat, weight):
    left = lanes(NQ) < XB
    for j in range(4):
        for pair in range(2):
            cols = slice(pair * 128, pair * 128 + 128)
            even = acc[2 * j * NQ : (2 * j + 1) * NQ, cols] * weight
            odd = acc[(2 * j + 1) * NQ : (2 * j + 2) * NQ, cols] * weight
            mat[j + 1, pl.ds(2 * pair, NQ, stride=ROWQ), :] = jnp.where(left, even, pltpu.roll(odd, XB, 1))
            mat[j + 1, pl.ds(2 * pair + 1, NQ, stride=ROWQ), :] = jnp.where(left, pltpu.roll(even, XB, 1), odd)


def cut_tiles(offs_ref, mat, tiles):
    lane = lanes(TR)
    for k in range(NTILES):
        t, q = k // 4, k % 4
        rows = slice(t * TR, t * TR + TR)
        off = offs_ref[0, k]
        side = jnp.where(off >= SHIFT, q + 2, q)
        turn = (128 + SHIFT - off) % 128
        own = pltpu.roll(mat[q + 1, rows, :], turn, 1)
        other = pltpu.roll(mat[side, rows, :], turn, 1)
        source = lane + (off - SHIFT)
        tiles[k] = jnp.where((source >= 0) & (source < 128), own, other)


def kernel(
    nz, npatch,
    offs_hbm, cell_hbm, coef_hbm, wgt_hbm, row_hbm, col_hbm, img_hbm, out_ref,
    offs, cell, coef, wgt, rowt, colt,
    buf, edge, scaled, phigh, plow, phi, plo, ehi, elo, acc, mat, tiles,
    slotv, slots, denx, denz, send, recv_x, xsum, recv_z,
    load_sem, slot_sem, halo_send, halo_recv, denx_send, denx_recv, denz_send, denz_recv,
    x_send, x_recv, z_send, z_recv, x_token, z_token,
):
    bounds = chunk_bounds(nz)
    me, patch = lax.axis_index("exp"), lax.axis_index("patch")
    zpos, xpos = me // NX, me % NX
    barrier = pltpu.get_barrier_semaphore()

    def along_x(n):
        return (zpos * NX + (xpos + n) % NX, patch)

    def at_z(z):
        return (z * NX + xpos, patch)

    def remote(src, dst, ssem, rsem, target):
        return pltpu.make_async_remote_copy(
            src_ref=src, dst_ref=dst, send_sem=ssem, recv_sem=rsem, device_id=target, device_id_type=MESH
        )

    def signal(sem, target):
        pl.semaphore_signal(sem, inc=1, device_id=target, device_id_type=MESH)

    def halo(way):
        source, target = ((NROWS - PAD, 8 * ROWQ), (0, 0))[way]
        return remote(
            buf.at[:, pl.ds(source, PAD), :],
            edge.at[:, pl.ds(target, PAD), :],
            halo_send.at[way],
            halo_recv.at[way],
            (me, patch + (1, -1)[way]),
        )

    def den_x(n):
        return remote(denx.at[0], denx.at[n], denx_send.at[n], denx_recv.at[n], along_x(n))

    def den_z(z, slot):
        return remote(denz.at[nz], denz.at[slot], denz_send.at[z], denz_recv.at[slot], at_z(z))

    def cells_x(n, g):
        rows = pl.ds(bounds[g], bounds[g + 1] - bounds[g])
        return remote(
            send.at[(xpos + n) % NX, rows], recv_x.at[n - 1, rows], x_send.at[n - 1, g], x_recv.at[n - 1, g], along_x(n)
        )

    def cells_z(z, slot):
        return remote(xsum.at[z], recv_z.at[slot], z_send.at[z], z_recv.at[slot], at_z(z))

    def others(action, start=0, stop=None):
        def one(z, carry):
            @pl.when(z != zpos)
            def _():
                action(z)

            return carry

        lax.fori_loop(start, nz if stop is None else stop, one, 0)

    def around(action):
        def one(d, carry):
            action((zpos + d) % nz)
            action((zpos + nz - d) % nz)
            return carry

        lax.fori_loop(1, nz // 2, one, 0)
        action((zpos + nz // 2) % nz)

    pairs = ((offs_hbm, offs), (cell_hbm, cell), (coef_hbm, coef), (wgt_hbm, wgt), (row_hbm, rowt), (col_hbm, colt))
    loads = [pltpu.make_async_copy(src, dst, load_sem.at[4 + k]) for k, (src, dst) in enumerate(pairs)]
    bands = [
        pltpu.make_async_copy(
            img_hbm.at[:, pl.ds(j * 128, 128)], buf.at[j], load_sem.at[j]
        )
        for j in range(4)
    ]
    for copy in loads + bands:
        copy.start()

    upper, lower = patch > 0, patch < npatch - 1

    @pl.when(upper)
    def _():
        signal(barrier, (me, patch - 1))

    @pl.when(lower)
    def _():
        signal(barrier, (me, patch + 1))

    for n in (1, NX - 1):
        signal(barrier, along_x(n))
    for d in (1, nz - 1):
        signal(barrier, at_z((zpos + d) % nz))

    gap = jnp.zeros((4, 8, 128), F32)
    edge[:, PAD : PAD + 8, :] = gap
    edge[:, EDGE * ROWQ - 8 :, :] = gap
    blank = jnp.zeros((ROWQ, NJ, 8, 128), F32)
    for plane, live in ((phi, NQ), (plo, NQ), (ehi, EDGE), (elo, EDGE)):
        plane[:, :, 0:8, :] = blank
        plane[:, :, live + 8 :, :] = blank
    mat[0] = jnp.zeros((NROWS, 128), F32)
    mat[5] = jnp.zeros((NROWS, 128), F32)
    tiles[NTILES] = jnp.zeros((TR, 128), F32)

    @pl.when(jnp.logical_not(upper))
    def _():
        edge[:, 8 * ROWQ : 8 * ROWQ + PAD, :] = jnp.zeros((4, PAD, 128), F32)

    @pl.when(jnp.logical_not(lower))
    def _():
        edge[:, 0:PAD, :] = jnp.zeros((4, PAD, 128), F32)

    for copy in loads:
        copy.wait()
    build_weights(coef, rowt, colt, scaled, phigh, plow)

    for copy in bands:
        copy.wait()
    pl.semaphore_wait(barrier, jnp.where(upper, 1, 0) + jnp.where(lower, 1, 0) + 4)

    @pl.when(lower)
    def _():
        halo(0).start()

    @pl.when(upper)
    def _():
        halo(1).start()

    for n in (1, NX - 1):
        signal(x_token, along_x(n))
    rounds = [1 << r for r in range(max(1, (nz // 2 - 1).bit_length()))]

    def greet(r):
        for d in (rounds[r], nz - rounds[r]):
            signal(z_token.at[r], at_z((zpos + d) % nz))

    greet(0)
    build_planes(NQ, 8, buf, phi, plo)
    lane = lanes(8)
    first = jnp.full((8, 128), NTILES, jnp.int32)
    last = jnp.full((8, 128), -1, jnp.int32)
    count = jnp.zeros((8, 128), F32)
    for k in range(NTILES):
        hit = lane == cell[0, k]
        count = count + jnp.where(hit, 1.0, 0.0)
        first = jnp.minimum(first, jnp.where(hit, k, NTILES))
        last = jnp.maximum(last, jnp.where(hit, k, -1))
    sub = lax.broadcasted_iota(jnp.int32, (8, 128), 0)
    slotv[...] = jnp.where(sub == 0, first, jnp.where(last > first, last, NTILES))
    slot_copy = pltpu.make_async_copy(slotv, slots, slot_sem)
    slot_copy.start()
    denx[0] = (count * wgt[0])[0:1]

    def relay(place):
        for r in range(1, len(rounds)):
            if RELAY[r - 1] == place:
                pl.semaphore_wait(z_token.at[r - 1], 2)
                greet(r)
        if RELAY[2] == place:
            pl.semaphore_wait(x_token, 2)
            for n in range(1, NX):
                den_x(n).start()

    convolve(range(0, MID), phi, plo, phigh, plow, acc)
    relay(0)
    convolve(range(MID, NA), phi, plo, phigh, plow, acc)
    relay(1)

    @pl.when(upper)
    def _():
        halo(0).wait_recv()

    @pl.when(lower)
    def _():
        halo(1).wait_recv()

    relay(2)
    build_planes(EDGE, 8, edge, ehi, elo)
    add_edges(ehi, elo, phigh, plow, acc)
    relay(3)
    to_matched(acc, mat, wgt[0])
    cut_tiles(offs, mat, tiles)
    slot_copy.wait()

    groups = len(bounds) - 1

    def send_x(g):
        for depth in range(bounds[g], bounds[g + 1]):
            for x in range(NX):
                place = depth * NX + x
                send[x, depth] = tiles[slots[0, place]] + tiles[slots[1, place]]
        for n in (2, 1, 3):
            cells_x(n, g).start()

    for g in range(min(AHEAD, groups)):
        send_x(g)
    relay(4)
    pl.semaphore_wait(z_token.at[len(rounds) - 1], 2)
    for n in range(1, NX):
        den_x(n).wait_recv()
    denz[nz] = denx[0] + denx[1] + denx[2] + denx[3]
    others(lambda z: den_z(z, zpos).start())

    for g in range(groups):
        for n in range(1, NX):
            cells_x(n, g).wait_recv()
        rows = pl.ds(bounds[g], bounds[g + 1] - bounds[g])
        xsum[rows] = (send[xpos, rows] + recv_x[0, rows]) + (recv_x[1, rows] + recv_x[2, rows])
        others(lambda z: cells_z(z, zpos).start(), bounds[g], bounds[g + 1])
        if g + AHEAD < groups:
            send_x(g + AHEAD)

    around(lambda z: den_z(z, z).wait_recv())
    denz[zpos] = denz[nz]
    den = denz[0]
    for z in range(1, nz):
        den = den + denz[z]
    den = jnp.sum(jnp.where(lanes(1) == me, den, 0.0), axis=1, keepdims=True)
    @pl.when(lower)
    def _():
        halo(0).wait_send()

    @pl.when(upper)
    def _():
        halo(1).wait_send()

    for n in range(1, NX):
        den_x(n).wait_send()
        for g in range(len(bounds) - 1):
            cells_x(n, g).wait_send()

    out_ref[...] = xsum[zpos]

    def add(z):
        cells_z(z, z).wait_recv()
        out_ref[...] += recv_z[z]

    around(add)
    out_ref[...] = out_ref[...] / den

    others(lambda z: den_z(z, zpos).wait_send())
    others(lambda z: cells_z(z, zpos).wait_send())


def per_device(nz, npatch, image, row_taps, col_taps, coefficients, exposure_weight, warp_offset, target_cell):
    hbm = pl.BlockSpec(memory_space=pltpu.HBM)
    vmem = pltpu.VMEM
    smem = pltpu.SMEM
    dma = pltpu.SemaphoreType.DMA
    rounds = max(1, (nz // 2 - 1).bit_length())
    out = pl.pallas_call(
        functools.partial(kernel, nz, npatch),
        out_shape=jax.ShapeDtypeStruct((TR, TW), F32),
        in_specs=[hbm] * 7,
        out_specs=pl.BlockSpec(memory_space=vmem),
        scratch_shapes=[
            smem((1, NTILES), jnp.int32),
            smem((1, NTILES), jnp.int32),
            smem((1, NB), F32),
            smem((1,), F32),
            vmem((NB, TAPS), F32),
            vmem((NB, TAPS), F32),
            vmem((4, NROWS, 128), F32),
            vmem((4, EDGE * ROWQ, 128), F32),
            vmem((NB, TAPS), F32),
            vmem(((NKAP + 2) * 128, 128), BF16),
            vmem(((NKAP + 2) * 128, 128), BF16),
            vmem((ROWQ, NJ, NG, 128), F32),
            vmem((ROWQ, NJ, NG, 128), F32),
            vmem((ROWQ, NJ, 2 * EDGE, 128), F32),
            vmem((ROWQ, NJ, 2 * EDGE, 128), F32),
            vmem((NJ * NQ, 256), F32),
            vmem((6, NROWS, 128), F32),
            vmem((NTILES + 1, TR, TW), F32),
            vmem((8, 128), jnp.int32),
            smem((8, 128), jnp.int32),
            vmem((NX, 1, 128), F32),
            vmem((nz + 1, 1, 128), F32),
            vmem((NX, nz, TR, TW), F32),
            vmem((NX - 1, nz, TR, TW), F32),
            vmem((nz, TR, TW), F32),
            vmem((nz, TR, TW), F32),
            dma((10,)),
            dma,
            dma((2,)),
            dma((2,)),
            dma((NX,)),
            dma((NX,)),
            dma((nz,)),
            dma((nz,)),
            dma((NX - 1, len(chunk_bounds(nz)) - 1)),
            dma((NX - 1, len(chunk_bounds(nz)) - 1)),
            dma((nz,)),
            dma((nz,)),
            pltpu.SemaphoreType.REGULAR,
            pltpu.SemaphoreType.REGULAR((rounds,)),
        ],
        compiler_params=pltpu.CompilerParams(
            collective_id=0, has_side_effects=True, vmem_limit_bytes=48 * 2**20
        ),
    )(
        *(
            part if part.size == 1 else pltpu.with_memory_space_constraint(part, pltpu.HBM)
            for part in (
                warp_offset.reshape(1, NTILES),
                target_cell.reshape(1, NTILES),
                coefficients,
                exposure_weight,
                row_taps,
                col_taps,
                image.reshape(NROWS, NCOLS),
            )
        )
    )
    return out[None, None]


def solution(mesh):
    nz = mesh.shape["exp"] // NX
    npatch = mesh.shape["patch"]
    return jax.shard_map(
        functools.partial(per_device, nz, npatch),
        mesh=mesh,
        in_specs=(
            P("exp", "patch", None),
            P(),
            P(),
            P("exp", None),
            P("exp"),
            P("exp", "patch", None),
            P("exp", "patch", None, None),
        ),
        out_specs=P("patch", "exp", None, None),
        check_vma=False,
    )
```

```python
import functools

import jax
import jax.numpy as jnp
from jax import lax
from jax.experimental import pallas as pl
from jax.experimental.pallas import tpu as pltpu
from jax.sharding import PartitionSpec as P

NB = 20
TAPS = 41
HALF = 20
NROWS = 128
NCOLS = 512
TR = 16
TW = 128
SHIFT = 8
NTILES = 32
NX = 4
PAD = 24
F32 = jnp.float32
BF16 = jnp.bfloat16
MESH = pl.DeviceIdType.MESH
ROWQ = 4
XB = 64
NJ = NCOLS // XB
NA = (ROWQ + TAPS + ROWQ - 2) // ROWQ
NKAP = NA * ROWQ
NQ = NROWS // ROWQ
NG = 48
EDGE = 16
MID = 5
RELAY = (1, 4, 1)
AHEAD = 9
BOUNDS = (0, 1, 2, 4, 6, 8, 10, 12, 14, 16)


def chunk_bounds(nz):
    return tuple(sorted({0, nz} | {max(1, nz * step // 16) for step in BOUNDS[1:]}))


def lanes(rows):
    return lax.broadcasted_iota(jnp.int32, (rows, 128), 1)


def build_weights(coef_ref, row_ref, col_ref, scaled, phigh, plow):
    for b in range(NB):
        scaled[b : b + 1, :] = col_ref[b : b + 1, :] * coef_ref[0, b]
    tap = lax.broadcasted_iota(jnp.int32, (TAPS, 128), 0)
    place = lax.broadcasted_iota(jnp.int32, (TAPS, 128), 1)
    flip = jnp.where((XB - place % XB) % XB == tap, 1.0, 0.0).astype(F32)
    rowpat = jnp.dot(row_ref[...], flip, precision=lax.Precision.HIGHEST, preferred_element_type=F32)
    pats = lax.dot_general(
        scaled[...], rowpat, (((0,), (0,)), ((), ())), precision=lax.Precision.HIGHEST, preferred_element_type=F32
    )
    left = lanes(XB) < XB
    gap = lax.broadcasted_iota(jnp.int32, (128, 128), 0) - lanes(128) % XB
    keep = (gap >= 0) & (gap < TAPS)
    zero = jnp.zeros((XB, 128), F32)
    rings = [zero] * (ROWQ - 1)
    for i in range(TAPS):
        base = jnp.broadcast_to(pats[i : i + 1, :], (XB, 128))
        rings.append(pltpu.roll(base, 0, 1, stride=1, stride_axis=0))
    rings += [zero] * ROWQ
    for kappa in range(-2, NKAP):
        pair = jnp.where(left, rings[kappa + 3], rings[kappa + 2])
        band = jnp.where(keep, jnp.concatenate([pair, pair], axis=0), 0.0)
        high = band.astype(BF16)
        rows = slice((kappa + 2) * 128, (kappa + 3) * 128)
        phigh[rows, :] = high
        plow[rows, :] = (band - high.astype(F32)).astype(BF16)


def build_planes(groups, base, buf, phi, plo):
    lane = lanes(groups)
    zero = jnp.zeros((groups, 128), F32)
    rows = slice(base, base + groups)
    for rho in range(ROWQ):
        cols = [buf[j, pl.ds(rho, groups, stride=ROWQ), :] for j in range(4)]
        near = [zero] + [pltpu.roll(part, HALF, 1) for part in cols]
        far = [pltpu.roll(part, XB + HALF, 1) for part in cols] + [zero]
        for j in range(4):
            even = jnp.where(lane < HALF, near[j], near[j + 1])
            odd = jnp.where(lane < XB + HALF, far[j], far[j + 1])
            for place, part in ((2 * j, even), (2 * j + 1, odd)):
                high = part.astype(BF16).astype(F32)
                phi[rho, place, rows, :] = high
                plo[rho, place, rows, :] = part - high


def products(a, start, rows, phi, plo, phigh, plow):
    def lhs(src):
        return jnp.concatenate(
            [
                jnp.concatenate([src[rho, j, start : start + rows, :].astype(BF16) for j in range(NJ)], axis=0)
                for rho in range(ROWQ)
            ],
            axis=1,
        )

    def rhs(src):
        return jnp.concatenate(
            [src[(a * ROWQ + 2) * 128 : (a * ROWQ + 6) * 128, :], src[a * ROWQ * 128 : (a * ROWQ + 4) * 128, :]], axis=1
        )

    def dot(x, y):
        return jnp.dot(x, y, preferred_element_type=F32)

    high, low = lhs(phi), lhs(plo)
    both = dot(jnp.concatenate([high, low], axis=0), rhs(phigh))
    return both[: NJ * rows] + both[NJ * rows :] + dot(high, rhs(plow))


def convolve(steps, phi, plo, phigh, plow, acc):
    for a in steps:
        part = products(a, a + 3, NQ, phi, plo, phigh, plow)
        if a == 0:
            acc[...] = part
        else:
            acc[...] += part


def add_edges(ehi, elo, phigh, plow, acc):
    reach = HALF // ROWQ
    tops = [products(a, EDGE + a + 1, 8, ehi, elo, phigh, plow) for a in range(reach)]
    ends = [products(a, a - 5, 8, ehi, elo, phigh, plow) for a in range(NA - reach, NA)]
    for parts, row in ((tops, 0), (ends, NQ - 8)):
        total = sum(parts[1:], parts[0])
        for j in range(NJ):
            acc[j * NQ + row : j * NQ + row + 8, :] += total[j * 8 : j * 8 + 8, :]


def to_matched(acc, mat, weight):
    left = lanes(NQ) < XB
    for j in range(4):
        for pair in range(2):
            cols = slice(pair * 128, pair * 128 + 128)
            even = acc[2 * j * NQ : (2 * j + 1) * NQ, cols] * weight
            odd = acc[(2 * j + 1) * NQ : (2 * j + 2) * NQ, cols] * weight
            mat[j + 1, pl.ds(2 * pair, NQ, stride=ROWQ), :] = jnp.where(left, even, pltpu.roll(odd, XB, 1))
            mat[j + 1, pl.ds(2 * pair + 1, NQ, stride=ROWQ), :] = jnp.where(left, pltpu.roll(even, XB, 1), odd)


def cut_tiles(offs_ref, mat, tiles):
    lane = lanes(TR)
    for k in range(NTILES):
        t, q = k // 4, k % 4
        rows = slice(t * TR, t * TR + TR)
        off = offs_ref[0, k]
        side = jnp.where(off >= SHIFT, q + 2, q)
        turn = (128 + SHIFT - off) % 128
        own = pltpu.roll(mat[q + 1, rows, :], turn, 1)
        other = pltpu.roll(mat[side, rows, :], turn, 1)
        source = lane + (off - SHIFT)
        tiles[k] = jnp.where((source >= 0) & (source < 128), own, other)


def kernel(
    nz, npatch,
    offs_hbm, cell_hbm, coef_hbm, wgt_hbm, row_hbm, col_hbm, img_hbm, out_ref,
    offs, cell, coef, wgt, rowt, colt,
    buf, edge, scaled, phigh, plow, phi, plo, ehi, elo, acc, mat, tiles,
    slotv, slots, denx, denz, send, recv_x, xsum, recv_z,
    load_sem, slot_sem, halo_send, halo_recv, denx_send, denx_recv, denz_send, denz_recv,
    x_send, x_recv, z_send, z_recv, x_token, z_token,
):
    bounds = chunk_bounds(nz)
    me, patch = lax.axis_index("exp"), lax.axis_index("patch")
    zpos, xpos = me // NX, me % NX
    barrier = pltpu.get_barrier_semaphore()

    def along_x(n):
        return (zpos * NX + (xpos + n) % NX, patch)

    def at_z(z):
        return (z * NX + xpos, patch)

    def remote(src, dst, ssem, rsem, target):
        return pltpu.make_async_remote_copy(
            src_ref=src, dst_ref=dst, send_sem=ssem, recv_sem=rsem, device_id=target, device_id_type=MESH
        )

    def signal(sem, target):
        pl.semaphore_signal(sem, inc=1, device_id=target, device_id_type=MESH)

    def halo(way):
        source, target = ((NROWS - PAD, 8 * ROWQ), (0, 0))[way]
        return remote(
            buf.at[:, pl.ds(source, PAD), :],
            edge.at[:, pl.ds(target, PAD), :],
            halo_send.at[way],
            halo_recv.at[way],
            (me, patch + (1, -1)[way]),
        )

    def den_x(n):
        return remote(denx.at[0], denx.at[n], denx_send.at[n], denx_recv.at[n], along_x(n))

    def den_z(z, slot):
        return remote(denz.at[nz], denz.at[slot], denz_send.at[z], denz_recv.at[slot], at_z(z))

    def cells_x(n, g):
        rows = pl.ds(bounds[g], bounds[g + 1] - bounds[g])
        return remote(
            send.at[(xpos + n) % NX, rows], recv_x.at[n - 1, rows], x_send.at[n - 1, g], x_recv.at[n - 1, g], along_x(n)
        )

    def cells_z(z, slot):
        return remote(xsum.at[z], recv_z.at[slot], z_send.at[z], z_recv.at[slot], at_z(z))

    def others(action, start=0, stop=None):
        def one(z, carry):
            @pl.when(z != zpos)
            def _():
                action(z)

            return carry

        lax.fori_loop(start, nz if stop is None else stop, one, 0)

    def around(action):
        def one(d, carry):
            action((zpos + d) % nz)
            action((zpos + nz - d) % nz)
            return carry

        lax.fori_loop(1, nz // 2, one, 0)
        action((zpos + nz // 2) % nz)

    pairs = ((offs_hbm, offs), (cell_hbm, cell), (coef_hbm, coef), (wgt_hbm, wgt), (row_hbm, rowt), (col_hbm, colt))
    loads = [pltpu.make_async_copy(src, dst, load_sem.at[4 + k]) for k, (src, dst) in enumerate(pairs)]
    bands = [
        pltpu.make_async_copy(
            img_hbm.at[:, pl.ds(j * 128, 128)], buf.at[j, pl.ds(0, NROWS), :], load_sem.at[j]
        )
        for j in range(4)
    ]
    for copy in loads + bands:
        copy.start()

    upper, lower = patch > 0, patch < npatch - 1

    @pl.when(upper)
    def _():
        signal(barrier, (me, patch - 1))

    @pl.when(lower)
    def _():
        signal(barrier, (me, patch + 1))

    for n in (1, NX - 1):
        signal(barrier, along_x(n))
    for d in (1, nz - 1):
        signal(barrier, at_z((zpos + d) % nz))

    gap = jnp.zeros((4, 8, 128), F32)
    edge[:, PAD : PAD + 8, :] = gap
    edge[:, EDGE * ROWQ - 8 : EDGE * ROWQ, :] = gap
    blank = jnp.zeros((ROWQ, NJ, 8, 128), F32)
    for plane, live in ((phi, NQ), (plo, NQ), (ehi, EDGE), (elo, EDGE)):
        plane[:, :, 0:8, :] = blank
        plane[:, :, live + 8 :, :] = blank
    mat[0, 0:NROWS, :] = jnp.zeros((NROWS, 128), F32)
    mat[5, 0:NROWS, :] = jnp.zeros((NROWS, 128), F32)
    tiles[NTILES] = jnp.zeros((TR, 128), F32)

    @pl.when(jnp.logical_not(upper))
    def _():
        edge[:, 8 * ROWQ : 8 * ROWQ + PAD, :] = jnp.zeros((4, PAD, 128), F32)

    @pl.when(jnp.logical_not(lower))
    def _():
        edge[:, 0:PAD, :] = jnp.zeros((4, PAD, 128), F32)

    for copy in loads:
        copy.wait()
    build_weights(coef, rowt, colt, scaled, phigh, plow)

    for copy in bands:
        copy.wait()
    pl.semaphore_wait(barrier, jnp.where(upper, 1, 0) + jnp.where(lower, 1, 0) + 4)

    @pl.when(lower)
    def _():
        halo(0).start()

    @pl.when(upper)
    def _():
        halo(1).start()

    for n in (1, NX - 1):
        signal(x_token, along_x(n))
    rounds = [1 << r for r in range(max(1, (nz // 2 - 1).bit_length()))]

    def greet(r):
        for d in (rounds[r], nz - rounds[r]):
            signal(z_token.at[r], at_z((zpos + d) % nz))

    greet(0)
    build_planes(NQ, 8, buf, phi, plo)
    lane = lanes(8)
    first = jnp.full((8, 128), NTILES, jnp.int32)
    last = jnp.full((8, 128), -1, jnp.int32)
    count = jnp.zeros((8, 128), F32)
    for k in range(NTILES):
        hit = lane == cell[0, k]
        count = count + jnp.where(hit, 1.0, 0.0)
        first = jnp.minimum(first, jnp.where(hit, k, NTILES))
        last = jnp.maximum(last, jnp.where(hit, k, -1))
    sub = lax.broadcasted_iota(jnp.int32, (8, 128), 0)
    slotv[...] = jnp.where(sub == 0, first, jnp.where(last > first, last, NTILES))
    slot_copy = pltpu.make_async_copy(slotv, slots, slot_sem)
    slot_copy.start()
    denx[0] = (count * wgt[0])[0:1]

    def relay(place):
        for r in range(1, len(rounds)):
            if RELAY[r - 1] == place:
                pl.semaphore_wait(z_token.at[r - 1], 2)
                greet(r)
        if RELAY[2] == place:
            pl.semaphore_wait(x_token, 2)
            for n in range(1, NX):
                den_x(n).start()

    convolve(range(0, MID), phi, plo, phigh, plow, acc)
    relay(0)
    convolve(range(MID, NA), phi, plo, phigh, plow, acc)
    relay(1)

    @pl.when(upper)
    def _():
        halo(0).wait_recv()

    @pl.when(lower)
    def _():
        halo(1).wait_recv()

    relay(2)
    build_planes(EDGE, 8, edge, ehi, elo)
    add_edges(ehi, elo, phigh, plow, acc)
    relay(3)
    to_matched(acc, mat, wgt[0])
    cut_tiles(offs, mat, tiles)
    slot_copy.wait()

    groups = len(bounds) - 1

    def send_x(g):
        for depth in range(bounds[g], bounds[g + 1]):
            for x in range(NX):
                place = depth * NX + x
                send[x, depth] = tiles[slots[0, place]] + tiles[slots[1, place]]
        for n in (2, 1, 3):
            cells_x(n, g).start()

    for g in range(min(AHEAD, groups)):
        send_x(g)
    relay(4)
    pl.semaphore_wait(z_token.at[len(rounds) - 1], 2)
    for n in range(1, NX):
        den_x(n).wait_recv()
    denz[nz] = denx[0] + denx[1] + denx[2] + denx[3]
    others(lambda z: den_z(z, zpos).start())

    for g in range(groups):
        for n in range(1, NX):
            cells_x(n, g).wait_recv()
        rows = pl.ds(bounds[g], bounds[g + 1] - bounds[g])
        xsum[rows] = (send[xpos, rows] + recv_x[0, rows]) + (recv_x[1, rows] + recv_x[2, rows])
        others(lambda z: cells_z(z, zpos).start(), bounds[g], bounds[g + 1])
        if g + AHEAD < groups:
            send_x(g + AHEAD)

    around(lambda z: den_z(z, z).wait_recv())
    denz[zpos] = denz[nz]
    den = denz[0]
    for z in range(1, nz):
        den = den + denz[z]
    den = jnp.sum(jnp.where(lanes(1) == me, den, 0.0), axis=1, keepdims=True)
    @pl.when(lower)
    def _():
        halo(0).wait_send()

    @pl.when(upper)
    def _():
        halo(1).wait_send()

    for n in range(1, NX):
        den_x(n).wait_send()
        for g in range(len(bounds) - 1):
            cells_x(n, g).wait_send()

    out_ref[...] = xsum[zpos]

    def add(z):
        cells_z(z, z).wait_recv()
        out_ref[...] += recv_z[z]

    around(add)
    out_ref[...] = out_ref[...] / den

    others(lambda z: den_z(z, zpos).wait_send())
    others(lambda z: cells_z(z, zpos).wait_send())


def per_device(nz, npatch, image, row_taps, col_taps, coefficients, exposure_weight, warp_offset, target_cell):
    hbm = pl.BlockSpec(memory_space=pltpu.HBM)
    vmem = pltpu.VMEM
    smem = pltpu.SMEM
    dma = pltpu.SemaphoreType.DMA
    rounds = max(1, (nz // 2 - 1).bit_length())
    out = pl.pallas_call(
        functools.partial(kernel, nz, npatch),
        out_shape=jax.ShapeDtypeStruct((TR, TW), F32),
        in_specs=[hbm] * 7,
        out_specs=pl.BlockSpec(memory_space=vmem),
        scratch_shapes=[
            smem((1, NTILES), jnp.int32),
            smem((1, NTILES), jnp.int32),
            smem((1, NB), F32),
            smem((1,), F32),
            vmem((NB, TAPS), F32),
            vmem((NB, TAPS), F32),
            vmem((4, NROWS + 8, 128), F32),
            vmem((4, EDGE * ROWQ + 8, 128), F32),
            vmem((NB, TAPS), F32),
            vmem(((NKAP + 2) * 128, 128), BF16),
            vmem(((NKAP + 2) * 128, 128), BF16),
            vmem((ROWQ, NJ, NG, 128), F32),
            vmem((ROWQ, NJ, NG, 128), F32),
            vmem((ROWQ, NJ, 2 * EDGE, 128), F32),
            vmem((ROWQ, NJ, 2 * EDGE, 128), F32),
            vmem((NJ * NQ, 256), F32),
            vmem((6, NROWS + 8, 128), F32),
            vmem((NTILES + 1, TR, TW), F32),
            vmem((8, 128), jnp.int32),
            smem((8, 128), jnp.int32),
            vmem((NX, 1, 128), F32),
            vmem((nz + 1, 1, 128), F32),
            vmem((NX, nz, TR, TW), F32),
            vmem((NX - 1, nz, TR, TW), F32),
            vmem((nz, TR, TW), F32),
            vmem((nz, TR, TW), F32),
            dma((10,)),
            dma,
            dma((2,)),
            dma((2,)),
            dma((NX,)),
            dma((NX,)),
            dma((nz,)),
            dma((nz,)),
            dma((NX - 1, len(chunk_bounds(nz)) - 1)),
            dma((NX - 1, len(chunk_bounds(nz)) - 1)),
            dma((nz,)),
            dma((nz,)),
            pltpu.SemaphoreType.REGULAR,
            pltpu.SemaphoreType.REGULAR((rounds,)),
        ],
        compiler_params=pltpu.CompilerParams(
            collective_id=0, has_side_effects=True, vmem_limit_bytes=48 * 2**20
        ),
    )(
        *(
            part if part.size == 1 else pltpu.with_memory_space_constraint(part, pltpu.HBM)
            for part in (
                warp_offset.reshape(1, NTILES),
                target_cell.reshape(1, NTILES),
                coefficients,
                exposure_weight,
                row_taps,
                col_taps,
                image.reshape(NROWS, NCOLS),
            )
        )
    )
    return out[None, None]


def solution(mesh):
    nz = mesh.shape["exp"] // NX
    npatch = mesh.shape["patch"]
    return jax.shard_map(
        functools.partial(per_device, nz, npatch),
        mesh=mesh,
        in_specs=(
            P("exp", "patch", None),
            P(),
            P(),
            P("exp", None),
            P("exp"),
            P("exp", "patch", None),
            P("exp", "patch", None, None),
        ),
        out_specs=P("patch", "exp", None, None),
        check_vma=False,
    )
```
